1024 devices in a mesh: lon: 64 (over x, y), lat: 16 (over z, core).
Axes of the slice: x: 8, y: 8, z: 8, core: 2. Of those that a mesh axis runs over, the one named last changes fastest.
Arguments:
- grid_latent: bfloat16 [256, 2048, 512], P('lat', 'lon'), may hold values from -6 to 6
- mesh_latent: bfloat16 [16, 64, 40, 512], P('lat', 'lon'), may hold values from -6 to 6
- grid_senders: int32 [16, 64, 1024], P('lat', 'lon'), may hold values from 0 to 835, as said below
- grid_targets: int32 [16, 64, 1024], P('lat', 'lon'), may hold values from 0 to 39
- grid_geometry: bfloat16 [16, 64, 4, 1024], P('lat', 'lon'), may hold values from -6 to 6
- mesh_senders: int32 [16, 64, 512], P('lat', 'lon'), may hold values from 0 to 1383, as said below
- mesh_targets: int32 [16, 64, 512], P('lat', 'lon'), may hold values from 0 to 39
- mesh_geometry: bfloat16 [16, 64, 4, 512], P('lat', 'lon'), may hold values from -6 to 6
- edge_counts: int32 [2, 16, 64], P(None, 'lat', 'lon'), may hold values from 128 to 1024, as said below
- encode_sender: bfloat16 [512, 512], replicated, may hold values from -0.25 to 0.25
- encode_target: bfloat16 [512, 512], replicated, may hold values from -0.25 to 0.25
- encode_geometry: bfloat16 [4, 512], replicated, may hold values from -3 to 3
- encode_output: bfloat16 [512, 512], replicated, may hold values from -0.25 to 0.25
- encode_self: bfloat16 [512, 512], replicated, may hold values from -0.25 to 0.25
- encode_inflow: bfloat16 [512, 512], replicated, may hold values from -0.25 to 0.25
- encode_final: bfloat16 [512, 512], replicated, may hold values from -0.25 to 0.25
- process_sender: bfloat16 [512, 512], replicated, may hold values from -1 to 1
- process_target: bfloat16 [512, 512], replicated, may hold values from -0.25 to 0.25
- process_geometry: bfloat16 [4, 512], replicated, may hold values from -3 to 3
- process_output: bfloat16 [512, 512], replicated, may hold values from -0.25 to 0.25
- process_self: bfloat16 [512, 512], replicated, may hold values from -0.25 to 0.25
- process_inflow: bfloat16 [512, 512], replicated, may hold values from -0.25 to 0.25
- process_final: bfloat16 [512, 512], replicated, may hold values from -0.25 to 0.25
Outputs:
- processed: bfloat16 [16, 64, 40, 512], P('lat', 'lon')
The draws below stay inside these ranges and needn't reach their ends.
Inputs may be any that keep to these rules, and one draw needn't show every extreme that they name: `grid_senders`: never names a grid row outside the grid: band 0 uses no r below 3, the last band no r at or above 19. `mesh_senders`: never names a neighbouring sector outside the latitude bands. `edge_counts`: multiples of 128, at least 128 and at most 1024 in row 0 and 512 in row 1; each row's capacity is reached by some sector in every draw.
All inputs are finite; a program needn't handle non-finite values.
Results may differ from the reference program's by a relative error of at most 0.013.
Values may be sent and summed in bfloat16 or wider, within the bound.
A program may use at most 32 MiB of HBM per device.

```python
import jax
import jax.numpy as jnp
from jax import lax

LATENT = 512
GEOMETRY = 4
GRID_LAT = 16
GRID_LON = 32
RIM_CELLS = 3
MESH_DEV = 40
GRID_EDGES = 1024
MESH_EDGES = 512
GRID_ROWS = 256
GRID_COLS = 2048
N_LON = 64
N_LAT = 16


def draw_grid_senders(key, part):
    key = jax.random.fold_in(key, 11)
    key_row, key_col = jax.random.split(key)
    ext_cols = GRID_LON + 2 * RIM_CELLS
    band_index = jnp.arange(N_LAT, dtype=jnp.int32)[:, None, None]
    low_row = jnp.where(band_index == 0, RIM_CELLS, 0)
    high_row = jnp.where(band_index == N_LAT - 1, GRID_LAT + RIM_CELLS, GRID_LAT + 2 * RIM_CELLS)
    shape = (N_LAT, N_LON, GRID_EDGES)
    cell_row = jax.random.randint(key_row, shape, low_row, high_row)
    cell_col = jax.random.randint(key_col, shape, 0, ext_cols)
    return (cell_row * ext_cols + cell_col).astype(jnp.int32)


def draw_mesh_senders(key, part):
    key = jax.random.fold_in(key, 23)
    key_row, key_col, key_slot, key_far, key_pick = jax.random.split(key, 5)
    band_index = jnp.arange(N_LAT, dtype=jnp.int32)[:, None, None]
    low_off = jnp.where(band_index == 0, 1, 0)
    high_off = jnp.where(band_index == N_LAT - 1, 2, 3)
    shape = (N_LAT, N_LON, MESH_EDGES)
    row_off = jax.random.randint(key_row, shape, low_off, high_off)
    col_off = jax.random.randint(key_col, shape, 0, 3)
    slot_index = jax.random.randint(key_slot, shape, 0, MESH_DEV)
    near_index = (row_off * 3 + col_off) * MESH_DEV + slot_index
    far_index = 9 * MESH_DEV + jax.random.randint(key_far, shape, 0, N_LAT * N_LON)
    picked = jax.random.randint(key_pick, shape, 0, 8)
    return jnp.where(picked < 5, far_index, near_index).astype(jnp.int32)


def draw_edge_counts(key, part):
    key = jax.random.fold_in(key, 37)
    band_index = jnp.arange(N_LAT, dtype=jnp.int32)[None, :, None]
    sector_lon = jnp.arange(N_LON, dtype=jnp.int32)[None, None, :]
    capacity = jnp.array([GRID_EDGES // 128, MESH_EDGES // 128], dtype=jnp.int32)[:, None, None]
    depth = jnp.minimum(band_index, N_LAT - 1 - band_index) + 1
    half_bands = (N_LAT + 1) // 2
    blocks = jnp.maximum(1, capacity * depth // half_bands)
    reduction = jax.random.randint(key, (2, N_LAT, N_LON), 0, 2) * (sector_lon % 2)
    return (128 * jnp.maximum(1, blocks - reduction)).astype(jnp.int32)


def draw_process_sender(key, part):
    key = jax.random.fold_in(key, 53)
    key_sign, key_off = jax.random.split(key)
    shape = (LATENT, LATENT)
    base = jnp.clip(jax.random.normal(key_off, shape, jnp.float32), -4.0, 4.0)
    skew = (base - base.T) * (0.3 / jnp.sqrt(2.0 * LATENT))
    signs = jnp.where(jax.random.bernoulli(key_sign, 0.5, (LATENT, 1)), 1.0, -1.0).astype(jnp.float32)
    rows = jnp.arange(LATENT, dtype=jnp.int32)[:, None]
    cols = jnp.arange(LATENT, dtype=jnp.int32)[None, :]
    identity = (rows == cols).astype(jnp.float32)
    return (signs * (identity + skew)).astype(jnp.bfloat16)


def touch_ends(values, key, low, high):
    dims = values.shape
    place = [jax.random.randint(jax.random.fold_in(key, axis), (), 0, dims[axis]) for axis in range(len(dims))]
    values = values.at[tuple(place)].set(low)
    longest = dims.index(max(dims))
    place[longest] = (place[longest] + 1) % dims[longest]
    return values.at[tuple(place)].set(high)


def block_scale(own_key, dims, cuts, smallest, high):
    def one(dim, blocks):
        steps = jax.random.uniform(jax.random.fold_in(jax.random.fold_in(own_key, 6), dim), (blocks,), jnp.float32, smallest / len(cuts), high / len(cuts))
        return jnp.repeat(jnp.exp(steps), dims[dim] // blocks).reshape((-1,) + (1,) * (len(dims) - dim - 1))

    factor_of = one(*cuts[0])
    for cut in cuts[1:]:
        factor_of = factor_of * one(*cut)
    return factor_of


def centred(rng, shape, scale, bound, pieces=(), held_as=jnp.bfloat16):
    entries = jax.random.normal(rng, shape, jnp.float32) * scale
    if len(pieces) > 0:
        entries = block_scale(rng, shape, pieces, -0.22, 0.18) * entries
    return jnp.clip(entries, min=-bound, max=bound).astype(held_as)


def setup_inputs(seed: int = 0) -> dict:
    arg_keys = jax.random.split(jax.random.key(seed), 24)
    grid_latent = centred(arg_keys[0], (GRID_ROWS, GRID_COLS, LATENT), 1.0, 6.0, ((0, 16), (1, 64)))
    mesh_latent = centred(arg_keys[1], (N_LAT, N_LON, MESH_DEV, LATENT), 1.0, 6.0, ((0, 16), (1, 64)))
    grid_senders = draw_grid_senders(jax.random.fold_in(arg_keys[23], 71), 0)
    grid_targets = touch_ends(jax.random.randint(arg_keys[3], (N_LAT, N_LON, GRID_EDGES), 0, MESH_DEV), jax.random.fold_in(arg_keys[3], 1), 0, MESH_DEV - 1).astype(jnp.int32)
    grid_geometry = centred(arg_keys[4], (N_LAT, N_LON, GEOMETRY, GRID_EDGES), 1.0, 6.0, ((0, 16), (1, 64)))
    mesh_senders = draw_mesh_senders(jax.random.fold_in(arg_keys[23], 71), 0)
    mesh_targets = touch_ends(jax.random.randint(arg_keys[6], (N_LAT, N_LON, MESH_EDGES), 0, MESH_DEV), jax.random.fold_in(arg_keys[6], 1), 0, MESH_DEV - 1).astype(jnp.int32)
    mesh_geometry = centred(arg_keys[7], (N_LAT, N_LON, GEOMETRY, MESH_EDGES), 1.0, 6.0, ((0, 16), (1, 64)))
    edge_counts = draw_edge_counts(jax.random.fold_in(arg_keys[23], 71), 0)
    encode_sender = centred(arg_keys[9], (LATENT, LATENT), LATENT ** -0.5, 0.25)
    encode_target = centred(arg_keys[10], (LATENT, LATENT), LATENT ** -0.5, 0.25)
    encode_geometry = centred(arg_keys[11], (GEOMETRY, LATENT), GEOMETRY ** -0.5, 3.0)
    encode_output = centred(arg_keys[12], (LATENT, LATENT), LATENT ** -0.5, 0.25)
    encode_self = centred(arg_keys[13], (LATENT, LATENT), LATENT ** -0.5, 0.25)
    encode_inflow = centred(arg_keys[14], (LATENT, LATENT), LATENT ** -0.5, 0.25)
    encode_final = centred(arg_keys[15], (LATENT, LATENT), LATENT ** -0.5, 0.25)
    process_sender = draw_process_sender(jax.random.fold_in(arg_keys[23], 71), 0)
    process_target = centred(arg_keys[17], (LATENT, LATENT), LATENT ** -0.5, 0.25)
    process_geometry = centred(arg_keys[18], (GEOMETRY, LATENT), GEOMETRY ** -0.5, 3.0)
    process_output = centred(arg_keys[19], (LATENT, LATENT), LATENT ** -0.5, 0.25)
    process_self = centred(arg_keys[20], (LATENT, LATENT), LATENT ** -0.5, 0.25)
    process_inflow = centred(arg_keys[21], (LATENT, LATENT), LATENT ** -0.5, 0.25)
    process_final = centred(arg_keys[22], (LATENT, LATENT), LATENT ** -0.5, 0.25)
    return {"grid_latent": grid_latent, "mesh_latent": mesh_latent, "grid_senders": grid_senders, "grid_targets": grid_targets, "grid_geometry": grid_geometry, "mesh_senders": mesh_senders, "mesh_targets": mesh_targets, "mesh_geometry": mesh_geometry, "edge_counts": edge_counts, "encode_sender": encode_sender, "encode_target": encode_target, "encode_geometry": encode_geometry, "encode_output": encode_output, "encode_self": encode_self, "encode_inflow": encode_inflow, "encode_final": encode_final, "process_sender": process_sender, "process_target": process_target, "process_geometry": process_geometry, "process_output": process_output, "process_self": process_self, "process_inflow": process_inflow, "process_final": process_final}


def layer_norm(values):
    centre = lax.optimization_barrier(jnp.mean(values, axis=-1, keepdims=True))
    shifted = values - centre
    spread = lax.optimization_barrier(jnp.mean(shifted * shifted, axis=-1, keepdims=True))
    return shifted * lax.rsqrt(spread + 1e-05)

def project(latent, weight):
    return jnp.dot(latent, weight, preferred_element_type=jnp.float32).astype(jnp.bfloat16)

def band_messages(sender_rows, targets, geometry, live_count, band_nodes, w_target, w_geometry, w_output):
    sector_count = band_nodes.shape[0]
    target_term = jnp.dot(band_nodes.reshape(-1, LATENT), w_target, preferred_element_type=jnp.float32)
    target_term = target_term.reshape(band_nodes.shape)
    target_rows = jnp.take_along_axis(target_term, targets[:, :, None], axis=1)
    geometry_term = jnp.einsum('lfe,fd->led', geometry.astype(jnp.float32), w_geometry.astype(jnp.float32))
    hidden = jax.nn.silu(geometry_term + sender_rows.astype(jnp.float32) + target_rows).astype(jnp.bfloat16)
    message = layer_norm(jnp.dot(hidden.reshape(-1, LATENT), w_output, preferred_element_type=jnp.float32))
    message = message.reshape(sector_count, -1, LATENT)
    edge_total = targets.shape[1]
    is_live = jnp.arange(edge_total, dtype=jnp.int32)[None, :] < live_count[:, None]
    message = jnp.where(is_live[:, :, None], message, 0.0)
    incidence = (targets[:, None, :] == jnp.arange(MESH_DEV, dtype=jnp.int32)[None, :, None]).astype(jnp.float32)
    return (message, incidence)

def node_update(band_nodes, message, incidence, w_self, w_inflow, w_final):
    inflow = jnp.einsum('lme,led->lmd', incidence, message, precision=lax.Precision.HIGHEST).astype(jnp.bfloat16)
    flat_nodes = band_nodes.reshape(-1, LATENT)
    inner_sum = jnp.dot(flat_nodes, w_self, preferred_element_type=jnp.float32)
    inner_sum = inner_sum + jnp.dot(inflow.reshape(-1, LATENT), w_inflow, preferred_element_type=jnp.float32)
    inner_hidden = jax.nn.silu(inner_sum).astype(jnp.bfloat16)
    update = layer_norm(jnp.dot(inner_hidden, w_final, preferred_element_type=jnp.float32))
    return (flat_nodes.astype(jnp.float32) + update).astype(jnp.bfloat16).reshape(band_nodes.shape)

def reference(grid_latent, mesh_latent, grid_senders, grid_targets, grid_geometry, mesh_senders, mesh_targets, mesh_geometry, edge_counts, encode_sender, encode_target, encode_geometry, encode_output, encode_self, encode_inflow, encode_final, process_sender, process_target, process_geometry, process_output, process_self, process_inflow, process_final):
    ext_cols = GRID_LON + 2 * RIM_CELLS
    grid_term = lax.map(lambda grid_row: project(grid_row, encode_sender), grid_latent)
    grid_term = grid_term.reshape(GRID_ROWS * GRID_COLS, LATENT)
    sector_lon = jnp.arange(N_LON, dtype=jnp.int32)[:, None]

    def encode_band(band_index):
        senders = grid_senders[band_index]
        cell_row = senders // ext_cols
        cell_col = senders % ext_cols
        global_row = band_index * GRID_LAT + cell_row - RIM_CELLS
        global_col = (sector_lon * GRID_LON + cell_col - RIM_CELLS) % GRID_COLS
        sender_rows = jnp.take(grid_term, (global_row * GRID_COLS + global_col).astype(jnp.int32), axis=0)
        band_nodes = mesh_latent[band_index]
        message, incidence = band_messages(sender_rows, grid_targets[band_index], grid_geometry[band_index], edge_counts[0, band_index], band_nodes, encode_target, encode_geometry, encode_output)
        return node_update(band_nodes, message, incidence, encode_self, encode_inflow, encode_final)
    encoded = lax.map(encode_band, jnp.arange(N_LAT, dtype=jnp.int32))
    mesh_term = project(encoded.reshape(-1, LATENT), process_sender)

    def process_band(band_index):
        senders = mesh_senders[band_index]
        is_near = senders < 9 * MESH_DEV
        block_index = senders // MESH_DEV
        slot_index = senders % MESH_DEV
        near_lat = band_index + block_index // 3 - 1
        near_lon = (sector_lon + block_index % 3 - 1) % N_LON
        far_index = senders - 9 * MESH_DEV
        far_lat = far_index % N_LAT
        far_lon = far_index // N_LAT
        node_index = jnp.where(is_near, (near_lat * N_LON + near_lon) * MESH_DEV + slot_index, (far_lat * N_LON + far_lon) * MESH_DEV)
        sender_rows = jnp.take(mesh_term, node_index.astype(jnp.int32), axis=0)
        band_nodes = encoded[band_index]
        message, incidence = band_messages(sender_rows, mesh_targets[band_index], mesh_geometry[band_index], edge_counts[1, band_index], band_nodes, process_target, process_geometry, process_output)
        return node_update(band_nodes, message, incidence, process_self, process_inflow, process_final)
    processed = lax.map(process_band, jnp.arange(N_LAT, dtype=jnp.int32))
    return processed
```

```python
import functools

import jax
import jax.numpy as jnp
from jax import lax
from jax.experimental import pallas as pl
from jax.experimental.pallas import tpu as pltpu
from jax.sharding import PartitionSpec as P

MESH = pl.DeviceIdType.MESH
LATENT = 512
HALF = 256
GRID_LAT = 16
GRID_LON = 32
RIM = 3
SLOTS = 40
BLOCK = 48
GRID_EDGES = 1024
MESH_EDGES = 512
TILE = 256
OWN = GRID_LAT * GRID_LON
UP, DOWN, LEFT, RIGHT = 0, 96, 192, 240
CORNER = 288
HALO = 384
PACKED = 160
GEO = 96
BF16, F32, I32 = jnp.bfloat16, jnp.float32, jnp.int32


def dot(a, b):
    return jnp.dot(a, b, preferred_element_type=F32)


def silu(v):
    half = 0.5 * v
    return half + half * jnp.tanh(half)


def layer_norm(v):
    centre = jnp.mean(v, axis=-1, keepdims=True)
    shifted = v - centre
    spread = jnp.mean(shifted * shifted, axis=-1, keepdims=True)
    return shifted * lax.rsqrt(spread + 1e-5)


def lanes(rows, columns):
    return lax.broadcasted_iota(I32, (rows, columns), 1).astype(F32)


def one_hot(column, width):
    return jnp.where(lanes(column.shape[0], width) == column, 1.0, 0.0).astype(BF16)


def target_hot(columns):
    place = lanes(columns.shape[0], 128)
    target = columns[:, 5:6]
    hot = jnp.where((place == target) | (place == target + BLOCK), 1.0, 0.0)
    for f in range(4):
        hot = jnp.where(place == GEO + f, columns[:, f : f + 1], hot)
    return hot.astype(BF16)


def fill_target_table(table, nodes, w_target, w_geometry):
    term = dot(nodes, w_target)
    high = term.astype(BF16)
    table[...] = jnp.zeros_like(table)
    table[0:SLOTS, :] = high
    table[BLOCK : BLOCK + SLOTS, :] = (term - high.astype(F32)).astype(BF16)
    table[GEO : GEO + 4, :] = w_geometry


def incidence(targets, count):
    edges = targets.shape[1]
    slot = lax.broadcasted_iota(I32, (SLOTS, edges), 0)
    live = lax.broadcasted_iota(I32, (SLOTS, edges), 1) < count
    return jnp.where((slot == targets) & live, 1.0, 0.0).astype(BF16)


def transposed(rows):
    return jnp.transpose(jnp.concatenate(rows, axis=0), (1, 0))


def kernel(nx, ny, nlat, *refs):
    (
        grid_hbm, mesh_hbm, gs_hbm, gt_hbm, gg_hbm, ms_hbm, mt_hbm, mg_hbm, ec_hbm,
        es_hbm, et_hbm, eg_hbm, eo_hbm, ei_hbm, ein_hbm, ef_hbm,
        ps_hbm, pt_hbm, pg_hbm, po_hbm, pi_hbm, pin_hbm, pf_hbm,
        out_ref,
        x_v, nodes_v, gs_v, gt_v, gg_v, ms_v, mt_v, mg_v, ec_v,
        es_v, et_v, eg_v, eo_v, ei_v, ein_v, ef_v,
        ps_v, pt_v, pg_v, po_v, pi_v, pin_v, pf_v,
        own_t, packed, halo_t, tg_t, columns_v, halo_hot, base, inc, inflow,
        near_t, near_mine, mtg_t, mcolumns_v, near_hot, far_hot0, far_hot1, mbase, minc, minflow,
        row_mine, rows_in, far_t,
        in_sem, halo_ss, halo_rs, near_ss, near_rs, s1_ss, s1_rs, s2_ss, s2_rs, s3_ss, s3_rs, s4_ss, s4_rs,
    ) = refs
    nlon = nx * ny
    lon, lat = lax.axis_index("lon"), lax.axis_index("lat")
    core = lax.rem(lat, 2)
    x, y = lon // ny, lax.rem(lon, ny)
    first = jnp.where(core == 0, x, y)
    second = jnp.where(core == 0, y, x)
    first_step = jnp.where(core == 0, ny, 1)
    second_step = jnp.where(core == 0, 1, ny)

    sources = [
        (grid_hbm, x_v), (es_hbm, es_v),
        (mesh_hbm.at[0, 0], nodes_v), (gs_hbm.at[0], gs_v), (gt_hbm.at[0], gt_v), (gg_hbm.at[0, 0], gg_v),
        (ec_hbm, ec_v), (et_hbm, et_v), (eg_hbm, eg_v), (eo_hbm, eo_v), (ei_hbm, ei_v), (ein_hbm, ein_v),
        (ef_hbm, ef_v), (ps_hbm, ps_v), (ms_hbm.at[0], ms_v), (mt_hbm.at[0], mt_v), (mg_hbm.at[0, 0], mg_v),
        (pt_hbm, pt_v), (pg_hbm, pg_v), (po_hbm, po_v), (pi_hbm, pi_v), (pin_hbm, pin_v), (pf_hbm, pf_v),
    ]
    loads = [pltpu.make_async_copy(src, dst, in_sem.at[k]) for k, (src, dst) in enumerate(sources)]
    for load in loads:
        load.start()

    def turn(v, step, n):
        return lax.rem(v + step + n, n)

    around = [(0, 1), (0, -1), (1, 0), (-1, 0), (1, 1), (1, -1), (-1, 1), (-1, -1)]

    def neighbour(step):
        return (turn(lon, step[1], nlon), turn(lat, step[0], nlat))

    def first_peer(k):
        return (lax.rem(first + k, nx) * first_step + second * second_step, lat)

    def second_peer(k):
        return (first * first_step + lax.rem(second + k, nx) * second_step, lat)

    barrier = pltpu.get_barrier_semaphore()

    def greet(device):
        pl.semaphore_signal(barrier, inc=1, device_id=device, device_id_type=MESH)

    for step in around:
        if step[1] != 0:
            greet(neighbour(step))

    def greet_line(k, carry):
        greet((lon, lax.rem(lat + k, nlat)))
        return carry

    def greet_plane(k, carry):
        greet(first_peer(k))
        greet(second_peer(k))
        return carry

    lax.fori_loop(1, nlat, greet_line, 0)
    lax.fori_loop(1, nx, greet_plane, 0)

    loads[0].wait()
    loads[1].wait()

    def project_own(i, carry):
        rows = x_v[pl.ds(i * (TILE // GRID_LON), TILE // GRID_LON)].reshape(TILE, LATENT)
        own_t[pl.ds(pl.multiple_of(i * TILE, TILE), TILE), :] = dot(rows, es_v[...]).astype(BF16)
        return carry

    lax.fori_loop(0, OWN // TILE, project_own, 0)
    place = lax.broadcasted_iota(I32, (PACKED, 128), 0)
    side = jnp.where(place < 48, place, place - 48)
    third = (side * 43) >> 7
    edge_row = third * GRID_LON + (side - 3 * third) + jnp.where(place < 48, GRID_LON - RIM, 0)
    corner = (place - 96) & 15
    which = (place - 96) >> 4
    third = (corner * 43) >> 7
    corner_row = (third + jnp.where(which < 2, GRID_LAT - RIM, 0)) * GRID_LON + (corner - 3 * third)
    corner_row = corner_row + jnp.where((which & 1) == 0, GRID_LON - RIM, 0)
    corner_row = jnp.where(corner < 9, corner_row, -1)
    wanted = jnp.where(place < 96, edge_row, corner_row)
    wanted = jnp.concatenate([wanted] * (OWN // 128), axis=1)
    pick = jnp.where(lax.broadcasted_iota(I32, (PACKED, OWN), 1) == wanted, 1.0, 0.0).astype(BF16)
    packed[...] = dot(pick, own_t[...]).astype(BF16)

    pl.semaphore_wait(barrier, (nlat - 1) + 2 * (nx - 1) + 6)

    halo_moves = [
        (packed.at[pl.ds(0, 48)], LEFT, 48, (0, 1)),
        (packed.at[pl.ds(48, 48)], RIGHT, 48, (0, -1)),
        (own_t.at[pl.ds(OWN - 96, 96)], UP, 96, (1, 0)),
        (own_t.at[pl.ds(0, 96)], DOWN, 96, (-1, 0)),
        (packed.at[pl.ds(96, 16)], CORNER, 16, (1, 1)),
        (packed.at[pl.ds(112, 16)], CORNER + 16, 16, (1, -1)),
        (packed.at[pl.ds(128, 16)], CORNER + 32, 16, (-1, 1)),
        (packed.at[pl.ds(144, 16)], CORNER + 48, 16, (-1, -1)),
    ]
    halo_copies = [
        pltpu.make_async_remote_copy(
            src_ref=src, dst_ref=halo_t.at[pl.ds(at, rows)], send_sem=halo_ss.at[k], recv_sem=halo_rs.at[k],
            device_id=neighbour(step), device_id_type=MESH,
        )
        for k, (src, at, rows, step) in enumerate(halo_moves)
    ]
    for copy in halo_copies:
        copy.start()

    for load in loads[2:13]:
        load.wait()
    halo_t[pl.ds(352, 32), :] = jnp.zeros((32, LATENT), BF16)
    nodes = nodes_v[...]
    fill_target_table(tg_t, nodes, et_v[...], eg_v[...])
    s = gs_v[...]
    r = (s * 1725) >> 16
    c = s - r * (GRID_LON + 2 * RIM)
    above, below = r < RIM, r >= GRID_LAT + RIM
    before, after = c < RIM, c >= GRID_LON + RIM
    row_in = jnp.where(above, r, jnp.where(below, r - GRID_LAT - RIM, r - RIM))
    col_in = jnp.where(before, c, jnp.where(after, c - GRID_LON - RIM, c - RIM))
    beside, over = before | after, above | below
    wide = row_in * GRID_LON + col_in
    thin = row_in * RIM + col_in
    own_at = jnp.where(beside | over, -1, wide)
    over_at = wide + jnp.where(above, UP, DOWN)
    beside_at = thin + jnp.where(before, LEFT, RIGHT)
    corner_at = thin + CORNER + jnp.where(above, 0, 32) + jnp.where(before, 0, 16)
    halo_at = jnp.where(over, jnp.where(beside, corner_at, over_at), jnp.where(beside, beside_at, -1))
    targets = gt_v[...]
    columns_v[...] = transposed([
        gg_v[...].astype(F32), own_at.astype(F32), targets.astype(F32), halo_at.astype(F32),
        jnp.zeros((1, GRID_EDGES), F32),
    ])
    inc[...] = incidence(targets, ec_v[0])
    inflow[...] = jnp.zeros_like(inflow)

    def grid_base(i, carry):
        edges = pl.ds(pl.multiple_of(i * TILE, TILE), TILE)
        columns = columns_v[edges, :]
        total = dot(one_hot(columns[:, 4:5], OWN), own_t[...])
        base[edges, :] = total + dot(target_hot(columns), tg_t[...])
        halo_hot[edges, :] = one_hot(columns[:, 6:7], HALO)
        return carry

    lax.fori_loop(0, GRID_EDGES // TILE, grid_base, 0)
    self_term = dot(nodes, ei_v[...])

    for copy in halo_copies:
        copy.wait_recv()

    def grid_edges(i, carry):
        edges = pl.ds(pl.multiple_of(i * TILE, TILE), TILE)
        hidden = silu(base[edges, :] + dot(halo_hot[edges, :], halo_t[...])).astype(BF16)
        message = layer_norm(dot(hidden, eo_v[...])).astype(BF16)
        inflow[...] += dot(inc[:, edges], message)
        return carry

    lax.fori_loop(0, GRID_EDGES // TILE, grid_edges, 0)
    hidden = silu(self_term + dot(inflow[...].astype(BF16), ein_v[...])).astype(BF16)
    encoded = (nodes.astype(F32) + layer_norm(dot(hidden, ef_v[...]))).astype(BF16)
    loads[13].wait()
    term = dot(encoded, ps_v[...]).astype(BF16)

    row_mine[...] = term.astype(F32)[0:1, :]

    def line_copy(k):
        return pltpu.make_async_remote_copy(
            src_ref=row_mine, dst_ref=rows_in.at[lat], send_sem=s1_ss.at[k], recv_sem=s1_rs.at[lat],
            device_id=(lon, lax.rem(lat + k, nlat)), device_id_type=MESH,
        )

    def line_arrival(k):
        source = lax.rem(lat + k, nlat)
        return pltpu.make_async_remote_copy(
            src_ref=row_mine, dst_ref=rows_in.at[source], send_sem=s1_ss.at[k], recv_sem=s1_rs.at[source],
            device_id=(lon, source), device_id_type=MESH,
        )

    def start_line(k, carry):
        line_copy(k).start()
        return carry

    lax.fori_loop(1, nlat, start_line, 0)

    near_mine[0:SLOTS, :] = term
    near_mine[SLOTS:BLOCK, :] = jnp.zeros((BLOCK - SLOTS, LATENT), BF16)
    near_copies = []
    for k, step in enumerate(around):
        at = ((1 - step[0]) * 3 + (1 - step[1])) * BLOCK
        copy = pltpu.make_async_remote_copy(
            src_ref=near_mine, dst_ref=near_t.at[pl.ds(at, BLOCK)], send_sem=near_ss.at[k], recv_sem=near_rs.at[k],
            device_id=neighbour(step), device_id_type=MESH,
        )
        copy.start()
        near_copies.append(copy)
    near_t[pl.ds(4 * BLOCK, BLOCK), :] = near_mine[...]
    near_t[pl.ds(9 * BLOCK, 512 - 9 * BLOCK), :] = jnp.zeros((512 - 9 * BLOCK, LATENT), BF16)

    for load in loads[14:23]:
        load.wait()
    fill_target_table(mtg_t, encoded, pt_v[...], pg_v[...])
    s = ms_v[...]
    near = s < 9 * SLOTS
    sector = (s * 1639) >> 16
    near_at = jnp.where(near, sector * BLOCK + (s - sector * SLOTS), -1)
    t = s - 9 * SLOTS
    plane, line = t // nlat, lax.rem(t, nlat)
    far_x, far_y = plane // ny, lax.rem(plane, ny)
    far_at0 = jnp.where(near, -1, (far_y * nx + far_x) * nlat + line)
    far_at1 = jnp.where(near, -1, t)
    targets = mt_v[...]
    mcolumns_v[...] = transposed([
        mg_v[...].astype(F32), near_at.astype(F32), targets.astype(F32), far_at0.astype(F32), far_at1.astype(F32),
    ])
    minc[...] = incidence(targets, ec_v[1])
    minflow[...] = jnp.zeros_like(minflow)

    def mesh_hot(i, carry):
        edges = pl.ds(pl.multiple_of(i * TILE, TILE), TILE)
        columns = mcolumns_v[edges, :]
        near_hot[edges, :] = one_hot(columns[:, 4:5], 512)
        mbase[edges, :] = dot(target_hot(columns), mtg_t[...])
        far_hot0[edges, :] = one_hot(columns[:, 6:7], nlon * nlat)
        far_hot1[edges, :] = one_hot(columns[:, 7:8], nlon * nlat)
        return carry

    lax.fori_loop(0, MESH_EDGES // TILE, mesh_hot, 0)
    mself_term = dot(encoded, pi_v[...])

    def wait_line(k, carry):
        line_arrival(k).wait_recv()
        return carry

    lax.fori_loop(1, nlat, wait_line, 0)
    line_row = lax.broadcasted_iota(I32, (nlat, LATENT), 0)
    block = jnp.where(line_row == lat, row_mine[...], 0.0)
    for k in range(nlat):
        block = jnp.where((line_row == k) & (lat != k), rows_in[k], block)
    half = jnp.where(core == 0, block[:, :HALF], block[:, HALF:])
    far_t[core, second, first] = half.astype(BF16)

    def stage2(k, source):
        at = far_t.at[core, second, source]
        return pltpu.make_async_remote_copy(
            src_ref=at, dst_ref=at, send_sem=s2_ss.at[k], recv_sem=s2_rs.at[source],
            device_id=first_peer(k), device_id_type=MESH,
        )

    def stage3(k, source):
        at = far_t.at[core, source]
        return pltpu.make_async_remote_copy(
            src_ref=at, dst_ref=at, send_sem=s3_ss.at[k], recv_sem=s3_rs.at[source],
            device_id=second_peer(k), device_id_type=MESH,
        )

    def stage4(half_of, source):
        at = far_t.at[half_of, source]
        return pltpu.make_async_remote_copy(
            src_ref=at, dst_ref=at, send_sem=s4_ss.at[source], recv_sem=s4_rs.at[source],
            device_id=(lon, lat + 1 - 2 * core), device_id_type=MESH,
        )

    for k in range(1, nx):
        stage2(k, first).start()
    for k in range(1, nx):
        stage2(k, lax.rem(first + k, nx)).wait_recv()

    for k in range(1, nx):
        stage3(k, second).start()
    stage4(core, second).start()

    for copy in near_copies:
        copy.wait_recv()

    def near_base(i, carry):
        edges = pl.ds(pl.multiple_of(i * TILE, TILE), TILE)
        mbase[edges, :] += dot(near_hot[edges, :], near_t[...])
        return carry

    lax.fori_loop(0, MESH_EDGES // TILE, near_base, 0)

    order = sorted(range(1, nx), key=lambda k: min(k, nx - k))
    for k in order:
        source = lax.rem(second + k, nx)
        stage3(k, source).wait_recv()
        stage4(core, source).start()
    for k in range(nx):
        stage4(1 - core, k).wait_recv()

    table0 = far_t[0].reshape(nlon * nlat, HALF)
    table1 = far_t[1].reshape(nlon * nlat, HALF)

    def mesh_edges(i, carry):
        edges = pl.ds(pl.multiple_of(i * TILE, TILE), TILE)
        far = jnp.concatenate([dot(far_hot0[edges, :], table0), dot(far_hot1[edges, :], table1)], axis=1)
        hidden = silu(mbase[edges, :] + far).astype(BF16)
        message = layer_norm(dot(hidden, po_v[...])).astype(BF16)
        minflow[...] += dot(minc[:, edges], message)
        return carry

    lax.fori_loop(0, MESH_EDGES // TILE, mesh_edges, 0)
    hidden = silu(mself_term + dot(minflow[...].astype(BF16), pin_v[...])).astype(BF16)
    update = layer_norm(dot(hidden, pf_v[...]))
    out_ref[0, 0] = (encoded.astype(F32) + update).astype(BF16)

    for copy in halo_copies:
        copy.wait_send()
    for copy in near_copies:
        copy.wait_send()

    def end_line(k, carry):
        line_copy(k).wait_send()
        return carry

    lax.fori_loop(1, nlat, end_line, 0)
    for k in range(1, nx):
        stage2(k, first).wait_send()
        stage3(k, second).wait_send()
    for k in range(nx):
        stage4(core, k).wait_send()


def body(nx, ny, nlat, *args):
    weight = pltpu.VMEM((LATENT, LATENT), BF16)
    narrow = pltpu.VMEM((4, LATENT), BF16)
    far = nx * ny * nlat
    dma = pltpu.SemaphoreType.DMA
    scratch = [
        pltpu.VMEM((GRID_LAT, GRID_LON, LATENT), BF16), pltpu.VMEM((SLOTS, LATENT), BF16),
        pltpu.VMEM((1, GRID_EDGES), I32), pltpu.VMEM((1, GRID_EDGES), I32), pltpu.VMEM((4, GRID_EDGES), BF16),
        pltpu.VMEM((1, MESH_EDGES), I32), pltpu.VMEM((1, MESH_EDGES), I32), pltpu.VMEM((4, MESH_EDGES), BF16),
        pltpu.VMEM((2, 1, 1), I32),
        weight, weight, narrow, weight, weight, weight, weight,
        weight, weight, narrow, weight, weight, weight, weight,
        pltpu.VMEM((OWN, LATENT), BF16), pltpu.VMEM((PACKED, LATENT), BF16), pltpu.VMEM((HALO, LATENT), BF16),
        pltpu.VMEM((128, LATENT), BF16), pltpu.VMEM((GRID_EDGES, 8), F32), pltpu.VMEM((GRID_EDGES, HALO), BF16),
        pltpu.VMEM((GRID_EDGES, LATENT), F32), pltpu.VMEM((SLOTS, GRID_EDGES), BF16), pltpu.VMEM((SLOTS, LATENT), F32),
        pltpu.VMEM((512, LATENT), BF16), pltpu.VMEM((BLOCK, LATENT), BF16),
        pltpu.VMEM((128, LATENT), BF16), pltpu.VMEM((MESH_EDGES, 8), F32), pltpu.VMEM((MESH_EDGES, 512), BF16),
        pltpu.VMEM((MESH_EDGES, far), BF16), pltpu.VMEM((MESH_EDGES, far), BF16),
        pltpu.VMEM((MESH_EDGES, LATENT), F32), pltpu.VMEM((SLOTS, MESH_EDGES), BF16), pltpu.VMEM((SLOTS, LATENT), F32),
        pltpu.VMEM((1, LATENT), F32), pltpu.VMEM((nlat, 1, LATENT), F32), pltpu.VMEM((2, nx, nx, nlat, HALF), BF16),
        dma((23,)), dma((8,)), dma((8,)), dma((8,)), dma((8,)), dma((nlat,)), dma((nlat,)),
        dma((nx,)), dma((nx,)), dma((nx,)), dma((nx,)), dma((nx,)), dma((nx,)),
    ]
    return pl.pallas_call(
        functools.partial(kernel, nx, ny, nlat),
        out_shape=jax.ShapeDtypeStruct((1, 1, SLOTS, LATENT), BF16),
        in_specs=[pl.BlockSpec(memory_space=pl.ANY)] * 23,
        out_specs=pl.BlockSpec(memory_space=pltpu.VMEM),
        scratch_shapes=scratch,
        compiler_params=pltpu.CompilerParams(collective_id=0, has_side_effects=True, vmem_limit_bytes=60 * 2**20),
        cost_estimate=pl.CostEstimate(flops=3 * 10**9, bytes_accessed=6 * 10**6, transcendentals=10**6),
    )(*args)


def solution(mesh):
    nlon, nlat = mesh.shape["lon"], mesh.shape["lat"]
    nx = round(nlon**0.5)
    return jax.shard_map(
        functools.partial(body, nx, nlon // nx, nlat),
        mesh=mesh,
        in_specs=(
            P("lat", "lon", None),
            P("lat", "lon", None, None),
            P("lat", "lon", None),
            P("lat", "lon", None),
            P("lat", "lon", None, None),
            P("lat", "lon", None),
            P("lat", "lon", None),
            P("lat", "lon", None, None),
            P(None, "lat", "lon"),
        )
        + (P(),) * 14,
        out_specs=P("lat", "lon", None, None),
        check_vma=False,
    )
```

```python
import functools

import jax
import jax.numpy as jnp
from jax import lax
from jax.experimental import pallas as pl
from jax.experimental.pallas import tpu as pltpu
from jax.sharding import PartitionSpec as P

MESH = pl.DeviceIdType.MESH
LATENT = 512
HALF = 256
GRID_LAT = 16
GRID_LON = 32
RIM = 3
SLOTS = 40
BLOCK = 48
GRID_EDGES = 1024
MESH_EDGES = 512
TILE = 256
OWN = GRID_LAT * GRID_LON
UP, DOWN, LEFT, RIGHT = 0, 96, 192, 240
CORNER = 288
HALO = 384
PACKED = 160
GEO = 96
BF16, F32, I32 = jnp.bfloat16, jnp.float32, jnp.int32


def dot(a, b):
    return jnp.dot(a, b, preferred_element_type=F32)


def silu(v):
    half = 0.5 * v
    return half + half * jnp.tanh(half)


def layer_norm(v):
    centre = jnp.mean(v, axis=-1, keepdims=True)
    shifted = v - centre
    spread = jnp.mean(shifted * shifted, axis=-1, keepdims=True)
    return shifted * lax.rsqrt(spread + 1e-5)


def lanes(rows, columns):
    return lax.broadcasted_iota(I32, (rows, columns), 1).astype(F32)


def one_hot(column, width):
    return jnp.where(lanes(column.shape[0], width) == column, 1.0, 0.0).astype(BF16)


def target_hot(columns):
    place = lanes(columns.shape[0], 128)
    target = columns[:, 5:6]
    hot = jnp.where((place == target) | (place == target + BLOCK), 1.0, 0.0)
    for f in range(4):
        hot = jnp.where(place == GEO + f, columns[:, f : f + 1], hot)
    return hot.astype(BF16)


def fill_target_table(table, nodes, w_target, w_geometry):
    term = dot(nodes, w_target)
    high = term.astype(BF16)
    table[...] = jnp.zeros_like(table)
    table[0:SLOTS, :] = high
    table[BLOCK : BLOCK + SLOTS, :] = (term - high.astype(F32)).astype(BF16)
    table[GEO : GEO + 4, :] = w_geometry


def incidence(targets, count):
    edges = targets.shape[1]
    slot = lax.broadcasted_iota(I32, (SLOTS, edges), 0)
    live = lax.broadcasted_iota(I32, (SLOTS, edges), 1) < count
    return jnp.where((slot == targets) & live, 1.0, 0.0).astype(BF16)


def transposed(rows):
    return jnp.transpose(jnp.concatenate(rows, axis=0), (1, 0))


def kernel(nx, ny, nlat, *refs):
    (
        grid_hbm, mesh_hbm, gs_hbm, gt_hbm, gg_hbm, ms_hbm, mt_hbm, mg_hbm, ec_hbm,
        es_hbm, et_hbm, eg_hbm, eo_hbm, ei_hbm, ein_hbm, ef_hbm,
        ps_hbm, pt_hbm, pg_hbm, po_hbm, pi_hbm, pin_hbm, pf_hbm,
        out_ref,
        x_v, nodes_v, gs_v, gt_v, gg_v, ms_v, mt_v, mg_v, ec_v,
        es_v, et_v, eg_v, eo_v, ei_v, ein_v, ef_v,
        ps_v, pt_v, pg_v, po_v, pi_v, pin_v, pf_v,
        own_t, packed, halo_t, tg_t, columns_v, halo_hot, base, inc, inflow,
        near_t, mtg_t, mcolumns_v, near_hot, far_hot, mbase, minc, minflow,
        row_mine, rows_in, far_t,
        in_sem, late_sem, halo_ss, halo_rs, near_ss, near_rs, s1_ss, s1_rs, s2_ss, s2_rs, s3_ss, s3_rs, s4_ss, s4_rs,
    ) = refs
    nlon, half_line = nx * ny, nlat // 2
    lon, lat = lax.axis_index("lon"), lax.axis_index("lat")
    core = lax.rem(lat, 2)
    x, y = lon // ny, lax.rem(lon, ny)
    first = jnp.where(core == 0, x, y)
    second = jnp.where(core == 0, y, x)
    first_step = jnp.where(core == 0, ny, 1)
    second_step = jnp.where(core == 0, 1, ny)
    group = lat // half_line
    other = 1 - group
    place_in_line = lax.rem(lat, half_line)
    has_above, has_below = lat > 0, lat < nlat - 1

    sources = [
        (grid_hbm, x_v), (es_hbm, es_v),
        (mesh_hbm.at[0, 0], nodes_v), (gs_hbm.at[0], gs_v), (gt_hbm.at[0], gt_v), (gg_hbm.at[0, 0], gg_v),
        (ec_hbm, ec_v), (et_hbm, et_v), (eg_hbm, eg_v), (eo_hbm, eo_v), (ei_hbm, ei_v), (ein_hbm, ein_v),
        (ef_hbm, ef_v), (ps_hbm, ps_v), (ms_hbm.at[0], ms_v), (mt_hbm.at[0], mt_v), (mg_hbm.at[0, 0], mg_v),
        (pt_hbm, pt_v), (pg_hbm, pg_v), (po_hbm, po_v), (pi_hbm, pi_v), (pin_hbm, pin_v), (pf_hbm, pf_v),
    ]
    loads = [pltpu.make_async_copy(src, dst, in_sem.at[k]) for k, (src, dst) in enumerate(sources)]
    loads[0].start()
    loads[1].start()

    around = [(0, 1), (0, -1), (1, 0), (-1, 0), (1, 1), (1, -1), (-1, 1), (-1, -1)]

    def neighbour(step):
        return (lax.rem(lon + step[1] + nlon, nlon), lat + step[0])

    def receives(step):
        return {0: None, 1: has_above, -1: has_below}[step[0]]

    def sends(step):
        return {0: None, 1: has_below, -1: has_above}[step[0]]

    def guarded(condition, act):
        if condition is None:
            act()
        else:
            pl.when(condition)(act)

    def first_peer(k):
        return (lax.rem(first + k, nx) * first_step + second * second_step, lat)

    def second_peer(k):
        return (first * first_step + lax.rem(second + k, nx) * second_step, lat)

    def group_mate(k):
        return group * half_line + lax.rem(place_in_line + k, half_line)

    barrier = pltpu.get_barrier_semaphore()

    def greet(device):
        pl.semaphore_signal(barrier, inc=1, device_id=device, device_id_type=MESH)

    for step in around:
        if step[1] != 0:
            guarded(sends(step), functools.partial(greet, neighbour(step)))

    @pl.when(lat == half_line)
    def _():
        greet((lon, half_line - 1))

    def greet_mate(k, carry):
        greet((lon, group_mate(k)))
        return carry

    def greet_upper(k, carry):
        greet((lon, half_line + k))
        return carry

    def greet_plane(k, carry):
        greet(first_peer(k))
        greet(second_peer(k))
        return carry

    lax.fori_loop(1, half_line, greet_mate, 0)
    lax.fori_loop(1, nx, greet_plane, 0)

    @pl.when(group == 0)
    def _():
        lax.fori_loop(0, half_line, greet_upper, 0)

    greetings = 2 + 2 * jnp.where(has_above, 1, 0) + 2 * jnp.where(has_below, 1, 0) + 2 * (nx - 1) + half_line - 1
    greetings = greetings + jnp.where(group == 1, half_line, jnp.where(lat == half_line - 1, 1, 0))

    loads[0].wait()
    loads[1].wait()
    for load in loads[2:14]:
        load.start()

    def project_own(i, carry):
        rows = x_v[pl.ds(i * (TILE // GRID_LON), TILE // GRID_LON)].reshape(TILE, LATENT)
        own_t[pl.ds(pl.multiple_of(i * TILE, TILE), TILE), :] = dot(rows, es_v[...]).astype(BF16)
        return carry

    lax.fori_loop(0, OWN // TILE, project_own, 0)
    place = lax.broadcasted_iota(I32, (PACKED, 128), 0)
    side = jnp.where(place < 48, place, place - 48)
    third = (side * 43) >> 7
    edge_row = third * GRID_LON + (side - 3 * third) + jnp.where(place < 48, GRID_LON - RIM, 0)
    corner = (place - 96) & 15
    which = (place - 96) >> 4
    third = (corner * 43) >> 7
    corner_row = (third + jnp.where(which < 2, GRID_LAT - RIM, 0)) * GRID_LON + (corner - 3 * third)
    corner_row = corner_row + jnp.where((which & 1) == 0, GRID_LON - RIM, 0)
    corner_row = jnp.where(corner < 9, corner_row, -1)
    wanted = jnp.where(place < 96, edge_row, corner_row)
    wanted = jnp.concatenate([wanted] * (OWN // 128), axis=1)
    pick = jnp.where(lax.broadcasted_iota(I32, (PACKED, OWN), 1) == wanted, 1.0, 0.0).astype(BF16)
    packed[...] = dot(pick, own_t[...]).astype(BF16)

    pl.semaphore_wait(barrier, greetings)

    halo_moves = [
        (packed.at[pl.ds(0, 48)], LEFT, 48, (0, 1)),
        (packed.at[pl.ds(48, 48)], RIGHT, 48, (0, -1)),
        (own_t.at[pl.ds(OWN - 96, 96)], UP, 96, (1, 0)),
        (own_t.at[pl.ds(0, 96)], DOWN, 96, (-1, 0)),
        (packed.at[pl.ds(96, 16)], CORNER, 16, (1, 1)),
        (packed.at[pl.ds(112, 16)], CORNER + 16, 16, (1, -1)),
        (packed.at[pl.ds(128, 16)], CORNER + 32, 16, (-1, 1)),
        (packed.at[pl.ds(144, 16)], CORNER + 48, 16, (-1, -1)),
    ]
    halo_copies = [
        pltpu.make_async_remote_copy(
            src_ref=src, dst_ref=halo_t.at[pl.ds(at, rows)], send_sem=halo_ss.at[k], recv_sem=halo_rs.at[k],
            device_id=neighbour(step), device_id_type=MESH,
        )
        for k, (src, at, rows, step) in enumerate(halo_moves)
    ]
    for copy, (*_, step) in zip(halo_copies, halo_moves):
        guarded(sends(step), copy.start)

    @pl.when(group == 1)
    def _():
        def report(k, carry):
            pl.semaphore_signal(late_sem, inc=1, device_id=(lon, k), device_id_type=MESH)
            return carry

        lax.fori_loop(0, half_line, report, 0)

    for load in loads[14:]:
        load.start()

    def no_sector(at, rows):
        halo_t[pl.ds(at, rows), :] = jnp.zeros((rows, LATENT), BF16)

    @pl.when(lat == 0)
    def _():
        no_sector(UP, 96)
        no_sector(CORNER, 32)
        near_t[pl.ds(0, 3 * BLOCK), :] = jnp.zeros((3 * BLOCK, LATENT), BF16)

    @pl.when(lat == nlat - 1)
    def _():
        no_sector(DOWN, 96)
        no_sector(CORNER + 32, 32)
        near_t[pl.ds(6 * BLOCK, 3 * BLOCK), :] = jnp.zeros((3 * BLOCK, LATENT), BF16)

    for load in loads[2:13]:
        load.wait()
    halo_t[pl.ds(352, 32), :] = jnp.zeros((32, LATENT), BF16)
    nodes = nodes_v[...]
    fill_target_table(tg_t, nodes, et_v[...], eg_v[...])
    s = gs_v[...]
    r = (s * 1725) >> 16
    c = s - r * (GRID_LON + 2 * RIM)
    above, below = r < RIM, r >= GRID_LAT + RIM
    before, after = c < RIM, c >= GRID_LON + RIM
    row_in = jnp.where(above, r, jnp.where(below, r - GRID_LAT - RIM, r - RIM))
    col_in = jnp.where(before, c, jnp.where(after, c - GRID_LON - RIM, c - RIM))
    beside, over = before | after, above | below
    wide = row_in * GRID_LON + col_in
    thin = row_in * RIM + col_in
    own_at = jnp.where(beside | over, -1, wide)
    over_at = wide + jnp.where(above, UP, DOWN)
    beside_at = thin + jnp.where(before, LEFT, RIGHT)
    corner_at = thin + CORNER + jnp.where(above, 0, 32) + jnp.where(before, 0, 16)
    halo_at = jnp.where(over, jnp.where(beside, corner_at, over_at), jnp.where(beside, beside_at, -1))
    targets = gt_v[...]
    columns_v[...] = transposed([
        gg_v[...].astype(F32), own_at.astype(F32), targets.astype(F32), halo_at.astype(F32),
        jnp.zeros((1, GRID_EDGES), F32),
    ])
    inc[...] = incidence(targets, ec_v[0, :, 0:1])
    inflow[...] = jnp.zeros_like(inflow)

    def grid_base(i, carry):
        edges = pl.ds(pl.multiple_of(i * TILE, TILE), TILE)
        columns = columns_v[edges, :]
        total = dot(one_hot(columns[:, 4:5], OWN), own_t[...])
        base[edges, :] = total + dot(target_hot(columns), tg_t[...])
        halo_hot[edges, :] = one_hot(columns[:, 6:7], HALO)
        return carry

    lax.fori_loop(0, GRID_EDGES // TILE, grid_base, 0)
    self_term = dot(nodes, ei_v[...])

    for copy, (*_, step) in zip(halo_copies, halo_moves):
        guarded(receives(step), copy.wait_recv)

    def grid_edges(i, carry):
        edges = pl.ds(pl.multiple_of(i * TILE, TILE), TILE)
        hidden = silu(base[edges, :] + dot(halo_hot[edges, :], halo_t[...])).astype(BF16)
        message = layer_norm(dot(hidden, eo_v[...])).astype(BF16)
        inflow[...] += dot(inc[:, edges], message)
        return carry

    lax.fori_loop(0, GRID_EDGES // TILE, grid_edges, 0)
    hidden = silu(self_term + dot(inflow[...].astype(BF16), ein_v[...])).astype(BF16)
    encoded = (nodes.astype(F32) + layer_norm(dot(hidden, ef_v[...]))).astype(BF16)
    loads[13].wait()
    term = dot(encoded, ps_v[...]).astype(BF16)

    row_mine[...] = term.astype(F32)[0:1, :]
    rows_in[lat] = term.astype(F32)[0:1, :]

    def line_copy(target):
        return pltpu.make_async_remote_copy(
            src_ref=row_mine, dst_ref=rows_in.at[lat], send_sem=s1_ss.at[target], recv_sem=s1_rs.at[lat],
            device_id=(lon, target), device_id_type=MESH,
        )

    def line_arrival(source):
        return pltpu.make_async_remote_copy(
            src_ref=row_mine, dst_ref=rows_in.at[source], send_sem=s1_ss.at[source], recv_sem=s1_rs.at[source],
            device_id=(lon, source), device_id_type=MESH,
        )

    def send_mate(k, carry):
        line_copy(group_mate(k)).start()
        return carry

    def send_other(k, carry):
        line_copy(other * half_line + k).start()
        return carry

    @pl.when(group == 1)
    def _():
        lax.fori_loop(0, half_line, send_other, 0)

    lax.fori_loop(1, half_line, send_mate, 0)

    near_t[pl.ds(4 * BLOCK, SLOTS), :] = term
    near_t[pl.ds(4 * BLOCK + SLOTS, BLOCK - SLOTS), :] = jnp.zeros((BLOCK - SLOTS, LATENT), BF16)
    near_t[pl.ds(9 * BLOCK, 512 - 9 * BLOCK), :] = jnp.zeros((512 - 9 * BLOCK, LATENT), BF16)
    near_moves = [(4, 3, 1, (0, 1)), (4, 5, 1, (0, -1)), (3, 0, 3, (1, 0)), (3, 6, 3, (-1, 0))]
    near_copies = [
        pltpu.make_async_remote_copy(
            src_ref=near_t.at[pl.ds(source * BLOCK, blocks * BLOCK)], dst_ref=near_t.at[pl.ds(at * BLOCK, blocks * BLOCK)],
            send_sem=near_ss.at[k], recv_sem=near_rs.at[k], device_id=neighbour(step), device_id_type=MESH,
        )
        for k, (source, at, blocks, step) in enumerate(near_moves)
    ]
    near_copies[0].start()
    near_copies[1].start()

    for load in loads[14:23]:
        load.wait()
    fill_target_table(mtg_t, encoded, pt_v[...], pg_v[...])
    s = ms_v[...]
    sectors = nlon * half_line
    near = s < 9 * SLOTS
    sector = (s * 1639) >> 16
    near_at = jnp.where(near, sector * BLOCK + (s - sector * SLOTS), -1)
    t = s - 9 * SLOTS
    plane, line = t // nlat, lax.rem(t, nlat)
    far_x, far_y = plane // ny, lax.rem(plane, ny)
    offset = (line // half_line) * sectors + lax.rem(line, half_line)
    far_at0 = jnp.where(near, -1, (far_y * nx + far_x) * half_line + offset)
    far_at1 = jnp.where(near, -1, plane * half_line + offset)
    targets = mt_v[...]
    mcolumns_v[...] = transposed([
        mg_v[...].astype(F32), near_at.astype(F32), targets.astype(F32), far_at0.astype(F32), far_at1.astype(F32),
    ])
    minc[...] = incidence(targets, ec_v[0, :, 1:2])
    minflow[...] = jnp.zeros_like(minflow)

    def mesh_hot(i, carry):
        edges = pl.ds(pl.multiple_of(i * TILE, TILE), TILE)
        columns = mcolumns_v[edges, :]
        near_hot[edges, :] = one_hot(columns[:, 4:5], 512)
        mbase[edges, :] = dot(target_hot(columns), mtg_t[...])
        for g in range(2):
            far_hot[0, g, edges, :] = one_hot(columns[:, 6:7] - g * sectors, sectors)
            far_hot[1, g, edges, :] = one_hot(columns[:, 7:8] - g * sectors, sectors)
        return carry

    lax.fori_loop(0, MESH_EDGES // TILE, mesh_hot, 0)
    mself_term = dot(encoded, pi_v[...])

    near_copies[0].wait_recv()
    near_copies[1].wait_recv()
    for k in (2, 3):
        guarded(sends(near_moves[k][3]), near_copies[k].start)

    def place_rows(which):
        row_at = lax.broadcasted_iota(I32, (half_line, LATENT), 0)
        block = jnp.zeros((half_line, LATENT), F32)
        for k in range(half_line):
            block = jnp.where(row_at == k, rows_in[which * half_line + k], block)
        half = jnp.where(core == 0, block[:, :HALF], block[:, HALF:])
        far_t[which, core, second, first] = half.astype(BF16)

    def stage2(turn, which, k, source):
        at = far_t.at[which, core, second, source]
        return pltpu.make_async_remote_copy(
            src_ref=at, dst_ref=at, send_sem=s2_ss.at[turn, k], recv_sem=s2_rs.at[turn, source],
            device_id=first_peer(k), device_id_type=MESH,
        )

    def stage3(turn, which, k, source):
        at = far_t.at[which, core, source]
        return pltpu.make_async_remote_copy(
            src_ref=at, dst_ref=at, send_sem=s3_ss.at[turn, k], recv_sem=s3_rs.at[turn, source],
            device_id=second_peer(k), device_id_type=MESH,
        )

    def stage4(turn, which, half_of, source):
        at = far_t.at[which, half_of, source]
        return pltpu.make_async_remote_copy(
            src_ref=at, dst_ref=at, send_sem=s4_ss.at[turn, source], recv_sem=s4_rs.at[turn, source],
            device_id=(lon, lat + 1 - 2 * core), device_id_type=MESH,
        )

    order = sorted(range(1, nx), key=lambda k: min(k, nx - k))

    def start2(turn, which):
        for k in range(1, nx):
            stage2(turn, which, k, first).start()

    def start3(turn, which):
        for k in range(1, nx):
            stage2(turn, which, k, lax.rem(first + k, nx)).wait_recv()
        for k in range(1, nx):
            stage3(turn, which, k, second).start()
        stage4(turn, which, core, second).start()

    def hand_on(turn, which):
        for k in order:
            source = lax.rem(second + k, nx)
            stage3(turn, which, k, source).wait_recv()
            stage4(turn, which, core, source).start()

    def wait4(turn, which):
        for k in range(nx):
            stage4(turn, which, 1 - core, k).wait_recv()

    def far_part(which, edges):
        parts = [dot(far_hot[h, which, edges, :], far_t[which, h].reshape(sectors, HALF)) for h in range(2)]
        return jnp.concatenate(parts, axis=1)

    def wait_mate(k, carry):
        line_arrival(group_mate(k)).wait_recv()
        return carry

    def wait_other(k, carry):
        line_arrival(other * half_line + k).wait_recv()
        return carry

    lax.fori_loop(1, half_line, wait_mate, 0)
    place_rows(group)
    start2(0, group)

    @pl.when(group == 0)
    def _():
        pl.semaphore_wait(late_sem, half_line)
        lax.fori_loop(0, half_line, send_other, 0)

    for k in (2, 3):
        guarded(receives(near_moves[k][3]), near_copies[k].wait_recv)

    def near_base(i, carry):
        edges = pl.ds(pl.multiple_of(i * TILE, TILE), TILE)
        mbase[edges, :] += dot(near_hot[edges, :], near_t[...])
        return carry

    lax.fori_loop(0, MESH_EDGES // TILE, near_base, 0)
    start3(0, group)
    lax.fori_loop(0, half_line, wait_other, 0)
    place_rows(other)
    start2(1, other)
    hand_on(0, group)
    start3(1, other)
    wait4(0, group)

    def far_base(i, carry):
        edges = pl.ds(pl.multiple_of(i * TILE, TILE), TILE)
        mbase[edges, :] += far_part(group, edges)
        return carry

    lax.fori_loop(0, MESH_EDGES // TILE, far_base, 0)
    hand_on(1, other)
    wait4(1, other)

    def mesh_edges(i, carry):
        edges = pl.ds(pl.multiple_of(i * TILE, TILE), TILE)
        hidden = silu(mbase[edges, :] + far_part(other, edges)).astype(BF16)
        message = layer_norm(dot(hidden, po_v[...])).astype(BF16)
        minflow[...] += dot(minc[:, edges], message)
        return carry

    lax.fori_loop(0, MESH_EDGES // TILE, mesh_edges, 0)
    hidden = silu(mself_term + dot(minflow[...].astype(BF16), pin_v[...])).astype(BF16)
    update = layer_norm(dot(hidden, pf_v[...]))
    out_ref[0, 0] = (encoded.astype(F32) + update).astype(BF16)

    for copy, (*_, step) in zip(halo_copies, halo_moves):
        guarded(sends(step), copy.wait_send)
    for copy, (*_, step) in zip(near_copies, near_moves):
        guarded(sends(step), copy.wait_send)

    def end_mate(k, carry):
        line_copy(group_mate(k)).wait_send()
        return carry

    def end_other(k, carry):
        line_copy(other * half_line + k).wait_send()
        return carry

    lax.fori_loop(1, half_line, end_mate, 0)
    lax.fori_loop(0, half_line, end_other, 0)
    for turn, which in ((0, group), (1, other)):
        for k in range(1, nx):
            stage2(turn, which, k, first).wait_send()
            stage3(turn, which, k, second).wait_send()
        for k in range(nx):
            stage4(turn, which, core, k).wait_send()


def body(nx, ny, nlat, *args):
    weight = pltpu.VMEM((LATENT, LATENT), BF16)
    narrow = pltpu.VMEM((4, LATENT), BF16)
    half_line = nlat // 2
    sectors = nx * ny * half_line
    dma = pltpu.SemaphoreType.DMA
    scratch = [
        pltpu.VMEM((GRID_LAT, GRID_LON, LATENT), BF16), pltpu.VMEM((SLOTS, LATENT), BF16),
        pltpu.VMEM((1, GRID_EDGES), I32), pltpu.VMEM((1, GRID_EDGES), I32), pltpu.VMEM((4, GRID_EDGES), BF16),
        pltpu.VMEM((1, MESH_EDGES), I32), pltpu.VMEM((1, MESH_EDGES), I32), pltpu.VMEM((4, MESH_EDGES), BF16),
        pltpu.VMEM((1, 1, 2), I32),
        weight, weight, narrow, weight, weight, weight, weight,
        weight, weight, narrow, weight, weight, weight, weight,
        pltpu.VMEM((OWN, LATENT), BF16), pltpu.VMEM((PACKED, LATENT), BF16), pltpu.VMEM((HALO, LATENT), BF16),
        pltpu.VMEM((128, LATENT), BF16), pltpu.VMEM((GRID_EDGES, 8), F32), pltpu.VMEM((GRID_EDGES, HALO), BF16),
        pltpu.VMEM((GRID_EDGES, LATENT), F32), pltpu.VMEM((SLOTS, GRID_EDGES), BF16), pltpu.VMEM((SLOTS, LATENT), F32),
        pltpu.VMEM((512, LATENT), BF16),
        pltpu.VMEM((128, LATENT), BF16), pltpu.VMEM((MESH_EDGES, 8), F32), pltpu.VMEM((MESH_EDGES, 512), BF16),
        pltpu.VMEM((2, 2, MESH_EDGES, sectors), BF16),
        pltpu.VMEM((MESH_EDGES, LATENT), F32), pltpu.VMEM((SLOTS, MESH_EDGES), BF16), pltpu.VMEM((SLOTS, LATENT), F32),
        pltpu.VMEM((1, LATENT), F32), pltpu.VMEM((nlat, 1, LATENT), F32), pltpu.VMEM((2, 2, nx, nx, half_line, HALF), BF16),
        dma((23,)), pltpu.SemaphoreType.REGULAR, dma((8,)), dma((8,)), dma((4,)), dma((4,)), dma((nlat,)), dma((nlat,)),
        dma((2, nx)), dma((2, nx)), dma((2, nx)), dma((2, nx)), dma((2, nx)), dma((2, nx)),
    ]
    return pl.pallas_call(
        functools.partial(kernel, nx, ny, nlat),
        out_shape=pltpu.VMEM((1, 1, SLOTS, LATENT), BF16),
        in_specs=[pl.BlockSpec(memory_space=pl.ANY)] * 23,
        out_specs=pl.BlockSpec(memory_space=pltpu.VMEM),
        scratch_shapes=scratch,
        compiler_params=pltpu.CompilerParams(collective_id=0, has_side_effects=True, vmem_limit_bytes=60 * 2**20),
        cost_estimate=pl.CostEstimate(flops=3 * 10**9, bytes_accessed=6 * 10**6, transcendentals=10**6),
    )(*args[:8], jnp.transpose(args[8], (1, 2, 0)), *args[9:])


def solution(mesh):
    nlon, nlat = mesh.shape["lon"], mesh.shape["lat"]
    nx = round(nlon**0.5)
    return jax.shard_map(
        functools.partial(body, nx, nlon // nx, nlat),
        mesh=mesh,
        in_specs=(
            P("lat", "lon", None),
            P("lat", "lon", None, None),
            P("lat", "lon", None),
            P("lat", "lon", None),
            P("lat", "lon", None, None),
            P("lat", "lon", None),
            P("lat", "lon", None),
            P("lat", "lon", None, None),
            P(None, "lat", "lon"),
        )
        + (P(),) * 14,
        out_specs=P("lat", "lon", None, None),
        check_vma=False,
    )
```

```python
import functools

import jax
import jax.numpy as jnp
from jax import lax
from jax.experimental import pallas as pl
from jax.experimental.pallas import tpu as pltpu
from jax.sharding import PartitionSpec as P

MESH = pl.DeviceIdType.MESH
LATENT = 512
HALF = 256
GRID_LAT = 16
GRID_LON = 32
RIM = 3
SLOTS = 40
BLOCK = 48
GRID_EDGES = 1024
MESH_EDGES = 512
TILE = 256
OWN = GRID_LAT * GRID_LON
UP, DOWN, LEFT, RIGHT = 0, 96, 192, 240
CORNER = 288
HALO = 384
PACKED = 160
GEO = 96
BF16, F32, I32 = jnp.bfloat16, jnp.float32, jnp.int32


def dot(a, b):
    return jnp.dot(a, b, preferred_element_type=F32)


def silu(v):
    half = 0.5 * v
    return half + half * jnp.tanh(half)


def layer_norm(v):
    centre = jnp.mean(v, axis=-1, keepdims=True)
    shifted = v - centre
    spread = jnp.mean(shifted * shifted, axis=-1, keepdims=True)
    return shifted * lax.rsqrt(spread + 1e-5)


def lanes(rows, columns):
    return lax.broadcasted_iota(I32, (rows, columns), 1).astype(F32)


def one_hot(column, width):
    return jnp.where(lanes(column.shape[0], width) == column, 1.0, 0.0).astype(BF16)


def target_hot(columns):
    place = lanes(columns.shape[0], 128)
    target = columns[:, 5:6]
    hot = jnp.where((place == target) | (place == target + BLOCK), 1.0, 0.0)
    for f in range(4):
        hot = jnp.where(place == GEO + f, columns[:, f : f + 1], hot)
    return hot.astype(BF16)


def fill_target_table(table, nodes, w_target, w_geometry):
    term = dot(nodes, w_target)
    high = term.astype(BF16)
    table[...] = jnp.zeros_like(table)
    table[0:SLOTS, :] = high
    table[BLOCK : BLOCK + SLOTS, :] = (term - high.astype(F32)).astype(BF16)
    table[GEO : GEO + 4, :] = w_geometry


def incidence(targets, count):
    edges = targets.shape[1]
    slot = lax.broadcasted_iota(I32, (SLOTS, edges), 0)
    live = lax.broadcasted_iota(I32, (SLOTS, edges), 1) < count
    return jnp.where((slot == targets) & live, 1.0, 0.0).astype(BF16)


def transposed(rows):
    return jnp.transpose(jnp.concatenate(rows, axis=0), (1, 0))


def kernel(nx, ny, nlat, *refs):
    (
        grid_hbm, mesh_hbm, gs_hbm, gt_hbm, gg_hbm, ms_hbm, mt_hbm, mg_hbm, ec_hbm,
        es_hbm, et_hbm, eg_hbm, eo_hbm, ei_hbm, ein_hbm, ef_hbm,
        ps_hbm, pt_hbm, pg_hbm, po_hbm, pi_hbm, pin_hbm, pf_hbm,
        out_ref,
        x_v, nodes_v, gs_v, gt_v, gg_v, ms_v, mt_v, mg_v, ec_v,
        es_v, et_v, eg_v, eo_v, ei_v, ein_v, ef_v,
        ps_v, pt_v, pg_v, po_v, pi_v, pin_v, pf_v,
        own_t, packed, halo_t, tg_t, columns_v, halo_hot, base, inc,
        near_t, mtg_t, mcolumns_v, near_hot, far_hot, mbase, minc,
        row_mine, rows_in, far_t,
        in_sem, late_mate, late_other, halo_ss, halo_rs, near_ss, near_rs, s1_ss, s1_rs, s2_ss, s2_rs, s3_ss, s3_rs, s4_ss, s4_rs,
    ) = refs
    nlon, half_line = nx * ny, nlat // 2
    lon, lat = lax.axis_index("lon"), lax.axis_index("lat")
    core = lax.rem(lat, 2)
    x, y = lon // ny, lax.rem(lon, ny)
    first = jnp.where(core == 0, x, y)
    second = jnp.where(core == 0, y, x)
    first_step = jnp.where(core == 0, ny, 1)
    second_step = jnp.where(core == 0, 1, ny)
    group = lat // half_line
    other = 1 - group
    place_in_line = lax.rem(lat, half_line)
    has_above, has_below = lat > 0, lat < nlat - 1

    sources = [
        (grid_hbm, x_v), (es_hbm, es_v),
        (et_hbm, et_v), (eg_hbm, eg_v), (mesh_hbm.at[0, 0], nodes_v), (gs_hbm.at[0], gs_v), (gt_hbm.at[0], gt_v),
        (gg_hbm.at[0, 0], gg_v), (ec_hbm, ec_v), (eo_hbm, eo_v),
        (ei_hbm, ei_v), (ein_hbm, ein_v), (ef_hbm, ef_v), (ps_hbm, ps_v),
        (ms_hbm.at[0], ms_v), (mt_hbm.at[0], mt_v), (mg_hbm.at[0, 0], mg_v),
        (pt_hbm, pt_v), (pg_hbm, pg_v), (po_hbm, po_v), (pi_hbm, pi_v), (pin_hbm, pin_v), (pf_hbm, pf_v),
    ]
    loads = [pltpu.make_async_copy(src, dst, in_sem.at[k]) for k, (src, dst) in enumerate(sources)]
    loads[0].start()
    loads[1].start()

    around = [(0, 1), (0, -1), (1, 0), (-1, 0), (1, 1), (1, -1), (-1, 1), (-1, -1)]

    def neighbour(step):
        return (lax.rem(lon + step[1] + nlon, nlon), lat + step[0])

    def receives(step):
        return {0: None, 1: has_above, -1: has_below}[step[0]]

    def sends(step):
        return {0: None, 1: has_below, -1: has_above}[step[0]]

    def guarded(condition, act):
        if condition is None:
            act()
        else:
            pl.when(condition)(act)

    def first_peer(k):
        return (lax.rem(first + k, nx) * first_step + second * second_step, lat)

    def second_peer(k):
        return (first * first_step + lax.rem(second + k, nx) * second_step, lat)

    barrier = pltpu.get_barrier_semaphore()

    def greet(device):
        pl.semaphore_signal(barrier, inc=1, device_id=device, device_id_type=MESH)

    for step in around:
        if step[1] != 0:
            guarded(sends(step), functools.partial(greet, neighbour(step)))

    @pl.when(has_above)
    def _():
        greet((lon, lat - 1))

    def greet_line(k, carry):
        greet((lon, k))
        return carry

    def greet_plane(k, carry):
        greet(first_peer(k))
        greet(second_peer(k))
        return carry

    lax.fori_loop(lat + 1, nlat, greet_line, 0)
    lax.fori_loop(1, nx, greet_plane, 0)
    greetings = 2 + 2 * jnp.where(has_above, 1, 0) + 3 * jnp.where(has_below, 1, 0) + 2 * (nx - 1) + lat

    place = lax.broadcasted_iota(I32, (PACKED, 128), 0)
    side = jnp.where(place < 48, place, place - 48)
    third = (side * 43) >> 7
    edge_row = third * GRID_LON + (side - 3 * third) + jnp.where(place < 48, GRID_LON - RIM, 0)
    corner = (place - 96) & 15
    which = (place - 96) >> 4
    third = (corner * 43) >> 7
    corner_row = (third + jnp.where(which < 2, GRID_LAT - RIM, 0)) * GRID_LON + (corner - 3 * third)
    corner_row = corner_row + jnp.where((which & 1) == 0, GRID_LON - RIM, 0)
    corner_row = jnp.where(corner < 9, corner_row, -1)
    wanted = jnp.where(place < 96, edge_row, corner_row)
    wanted = jnp.concatenate([wanted] * (OWN // 128), axis=1)
    pick = jnp.where(lax.broadcasted_iota(I32, (PACKED, OWN), 1) == wanted, 1.0, 0.0).astype(BF16)
    loads[0].wait()
    loads[1].wait()
    for load in loads[2:10]:
        load.start()
    own_t[...] = dot(x_v[...].reshape(OWN, LATENT), es_v[...]).astype(BF16)
    packed[...] = dot(pick, own_t[...]).astype(BF16)

    pl.semaphore_wait(barrier, greetings)

    halo_moves = [
        (packed.at[pl.ds(0, 48)], LEFT, 48, (0, 1)),
        (packed.at[pl.ds(48, 48)], RIGHT, 48, (0, -1)),
        (own_t.at[pl.ds(OWN - 96, 96)], UP, 96, (1, 0)),
        (own_t.at[pl.ds(0, 96)], DOWN, 96, (-1, 0)),
        (packed.at[pl.ds(96, 16)], CORNER, 16, (1, 1)),
        (packed.at[pl.ds(112, 16)], CORNER + 16, 16, (1, -1)),
        (packed.at[pl.ds(128, 16)], CORNER + 32, 16, (-1, 1)),
        (packed.at[pl.ds(144, 16)], CORNER + 48, 16, (-1, -1)),
    ]
    halo_copies = [
        pltpu.make_async_remote_copy(
            src_ref=src, dst_ref=halo_t.at[pl.ds(at, rows)], send_sem=halo_ss.at[k], recv_sem=halo_rs.at[k],
            device_id=neighbour(step), device_id_type=MESH,
        )
        for k, (src, at, rows, step) in enumerate(halo_moves)
    ]
    for copy, (*_, step) in zip(halo_copies, halo_moves):
        guarded(sends(step), copy.start)

    for load in loads[10:]:
        load.start()

    def report_mate(k, carry):
        pl.semaphore_signal(late_mate, inc=1, device_id=(lon, k), device_id_type=MESH)
        return carry

    def report_other(k, carry):
        pl.semaphore_signal(late_other, inc=1, device_id=(lon, k), device_id_type=MESH)
        return carry

    lax.fori_loop(group * half_line, lat, report_mate, 0)
    lax.fori_loop(0, group * half_line, report_other, 0)

    def no_sector(at, rows):
        halo_t[pl.ds(at, rows), :] = jnp.zeros((rows, LATENT), BF16)

    @pl.when(lat == 0)
    def _():
        no_sector(UP, 96)
        no_sector(CORNER, 32)
        near_t[pl.ds(0, 3 * BLOCK), :] = jnp.zeros((3 * BLOCK, LATENT), BF16)

    @pl.when(lat == nlat - 1)
    def _():
        no_sector(DOWN, 96)
        no_sector(CORNER + 32, 32)
        near_t[pl.ds(6 * BLOCK, 3 * BLOCK), :] = jnp.zeros((3 * BLOCK, LATENT), BF16)

    for load in loads[2:10]:
        load.wait()
    halo_t[pl.ds(352, 32), :] = jnp.zeros((32, LATENT), BF16)
    nodes = nodes_v[...]
    fill_target_table(tg_t, nodes, et_v[...], eg_v[...])
    s = gs_v[...]
    r = (s * 1725) >> 16
    c = s - r * (GRID_LON + 2 * RIM)
    above, below = r < RIM, r >= GRID_LAT + RIM
    before, after = c < RIM, c >= GRID_LON + RIM
    row_in = jnp.where(above, r, jnp.where(below, r - GRID_LAT - RIM, r - RIM))
    col_in = jnp.where(before, c, jnp.where(after, c - GRID_LON - RIM, c - RIM))
    beside, over = before | after, above | below
    wide = row_in * GRID_LON + col_in
    thin = row_in * RIM + col_in
    own_at = jnp.where(beside | over, -1, wide)
    over_at = wide + jnp.where(above, UP, DOWN)
    beside_at = thin + jnp.where(before, LEFT, RIGHT)
    corner_at = thin + CORNER + jnp.where(above, 0, 32) + jnp.where(before, 0, 16)
    halo_at = jnp.where(over, jnp.where(beside, corner_at, over_at), jnp.where(beside, beside_at, -1))
    targets = gt_v[...]
    columns_v[...] = transposed([
        gg_v[...].astype(F32), own_at.astype(F32), targets.astype(F32), halo_at.astype(F32),
        jnp.zeros((1, GRID_EDGES), F32),
    ])
    inc[...] = incidence(targets, ec_v[0, :, 0:1])

    def grid_base(i, carry):
        edges = pl.ds(pl.multiple_of(i * TILE, TILE), TILE)
        columns = columns_v[edges, :]
        total = dot(one_hot(columns[:, 4:5], OWN), own_t[...])
        base[edges, :] = total + dot(target_hot(columns), tg_t[...])
        halo_hot[edges, :] = one_hot(columns[:, 6:7], HALO)
        return carry

    lax.fori_loop(0, GRID_EDGES // TILE, grid_base, 0, unroll=True)
    for load in loads[10:14]:
        load.wait()
    self_term = dot(nodes, ei_v[...])

    for copy, (*_, step) in zip(halo_copies, halo_moves):
        guarded(receives(step), copy.wait_recv)

    hidden = silu(base[...] + dot(halo_hot[...], halo_t[...])).astype(BF16)
    message = layer_norm(dot(hidden, eo_v[...])).astype(BF16)
    inflow = dot(inc[...], message).astype(BF16)
    hidden = silu(self_term + dot(inflow, ein_v[...])).astype(BF16)
    encoded = (nodes.astype(F32) + layer_norm(dot(hidden, ef_v[...]))).astype(BF16)
    term = dot(encoded, ps_v[...]).astype(BF16)

    row_mine[...] = term.astype(F32)[0:1, :]
    rows_in[lat] = term.astype(F32)[0:1, :]

    def line_copy(target):
        return pltpu.make_async_remote_copy(
            src_ref=row_mine, dst_ref=rows_in.at[lat], send_sem=s1_ss.at[target], recv_sem=s1_rs.at[lat],
            device_id=(lon, target), device_id_type=MESH,
        )

    def line_arrival(source):
        return pltpu.make_async_remote_copy(
            src_ref=row_mine, dst_ref=rows_in.at[source], send_sem=s1_ss.at[source], recv_sem=s1_rs.at[source],
            device_id=(lon, source), device_id_type=MESH,
        )

    def send_row(k, carry):
        line_copy(k).start()
        return carry

    lax.fori_loop(0, lat, send_row, 0)

    @pl.when(place_in_line < half_line - 1)
    def _():
        pl.semaphore_wait(late_mate, half_line - 1 - place_in_line)

    lax.fori_loop(lat + 1, (group + 1) * half_line, send_row, 0)

    near_t[pl.ds(4 * BLOCK, SLOTS), :] = term
    near_t[pl.ds(4 * BLOCK + SLOTS, BLOCK - SLOTS), :] = jnp.zeros((BLOCK - SLOTS, LATENT), BF16)
    near_t[pl.ds(9 * BLOCK, 512 - 9 * BLOCK), :] = jnp.zeros((512 - 9 * BLOCK, LATENT), BF16)
    near_moves = [(4, 3, 1, (0, 1)), (4, 5, 1, (0, -1)), (3, 0, 3, (1, 0)), (3, 6, 3, (-1, 0))]
    near_copies = [
        pltpu.make_async_remote_copy(
            src_ref=near_t.at[pl.ds(source * BLOCK, blocks * BLOCK)], dst_ref=near_t.at[pl.ds(at * BLOCK, blocks * BLOCK)],
            send_sem=near_ss.at[k], recv_sem=near_rs.at[k], device_id=neighbour(step), device_id_type=MESH,
        )
        for k, (source, at, blocks, step) in enumerate(near_moves)
    ]
    near_copies[0].start()
    near_copies[1].start()

    for load in loads[14:23]:
        load.wait()
    fill_target_table(mtg_t, encoded, pt_v[...], pg_v[...])
    s = ms_v[...]
    sectors = nlon * half_line
    near = s < 9 * SLOTS
    sector = (s * 1639) >> 16
    near_at = jnp.where(near, sector * BLOCK + (s - sector * SLOTS), -1)
    t = s - 9 * SLOTS
    plane, line = t // nlat, lax.rem(t, nlat)
    far_x, far_y = plane // ny, lax.rem(plane, ny)
    offset = (line // half_line) * sectors + lax.rem(line, half_line)
    far_at0 = jnp.where(near, -1, (far_y * nx + far_x) * half_line + offset)
    far_at1 = jnp.where(near, -1, plane * half_line + offset)
    targets = mt_v[...]
    mcolumns_v[...] = transposed([
        mg_v[...].astype(F32), near_at.astype(F32), targets.astype(F32), far_at0.astype(F32), far_at1.astype(F32),
    ])
    minc[...] = incidence(targets, ec_v[0, :, 1:2])

    columns = mcolumns_v[...]
    near_hot[...] = one_hot(columns[:, 4:5], 512)
    mbase[...] = dot(target_hot(columns), mtg_t[...])
    for g in range(2):
        far_hot[0, g] = one_hot(columns[:, 6:7] - g * sectors, sectors)
        far_hot[1, g] = one_hot(columns[:, 7:8] - g * sectors, sectors)
    mself_term = dot(encoded, pi_v[...])

    near_copies[0].wait_recv()
    near_copies[1].wait_recv()
    for k in (2, 3):
        guarded(sends(near_moves[k][3]), near_copies[k].start)

    def place_rows(which):
        row_at = lax.broadcasted_iota(I32, (half_line, LATENT), 0)
        block = jnp.zeros((half_line, LATENT), F32)
        for k in range(half_line):
            block = jnp.where(row_at == k, rows_in[which * half_line + k], block)
        half = jnp.where(core == 0, block[:, :HALF], block[:, HALF:])
        far_t[which, core, second, first] = half.astype(BF16)

    def stage2(turn, which, k, source):
        at = far_t.at[which, core, second, source]
        return pltpu.make_async_remote_copy(
            src_ref=at, dst_ref=at, send_sem=s2_ss.at[turn, k], recv_sem=s2_rs.at[turn, source],
            device_id=first_peer(k), device_id_type=MESH,
        )

    def stage3(turn, which, k, source):
        at = far_t.at[which, core, source]
        return pltpu.make_async_remote_copy(
            src_ref=at, dst_ref=at, send_sem=s3_ss.at[turn, k], recv_sem=s3_rs.at[turn, source],
            device_id=second_peer(k), device_id_type=MESH,
        )

    def stage4(turn, which, half_of, source):
        at = far_t.at[which, half_of, source]
        return pltpu.make_async_remote_copy(
            src_ref=at, dst_ref=at, send_sem=s4_ss.at[turn, source], recv_sem=s4_rs.at[turn, source],
            device_id=(lon, lat + 1 - 2 * core), device_id_type=MESH,
        )

    order = sorted(range(1, nx), key=lambda k: min(k, nx - k))

    def start2(turn, which):
        for k in range(1, nx):
            stage2(turn, which, k, first).start()

    def start3(turn, which):
        for k in range(1, nx):
            stage2(turn, which, k, lax.rem(first + k, nx)).wait_recv()
        for k in range(1, nx):
            stage3(turn, which, k, second).start()
        stage4(turn, which, core, second).start()

    def hand_on(turn, which):
        for k in order:
            source = lax.rem(second + k, nx)
            stage3(turn, which, k, source).wait_recv()
            stage4(turn, which, core, source).start()

    def wait4(turn, which):
        for k in range(nx):
            stage4(turn, which, 1 - core, k).wait_recv()

    def far_part(which):
        parts = [dot(far_hot[h, which], far_t[which, h].reshape(sectors, HALF)) for h in range(2)]
        return jnp.concatenate(parts, axis=1)

    def wait_row(k, carry):
        line_arrival(k).wait_recv()
        return carry

    lax.fori_loop(group * half_line, lat, wait_row, 0)
    lax.fori_loop(lat + 1, (group + 1) * half_line, wait_row, 0)
    place_rows(group)
    start2(0, group)

    @pl.when(group == 0)
    def _():
        pl.semaphore_wait(late_other, half_line)
        lax.fori_loop(half_line, nlat, send_row, 0)

    for k in (2, 3):
        guarded(receives(near_moves[k][3]), near_copies[k].wait_recv)
    mbase[...] += dot(near_hot[...], near_t[...])
    lax.fori_loop(other * half_line, (other + 1) * half_line, wait_row, 0)
    place_rows(other)
    start2(1, other)
    start3(0, group)
    start3(1, other)
    hand_on(0, group)
    wait4(0, group)
    mbase[...] += far_part(group)
    hand_on(1, other)
    wait4(1, other)
    hidden = silu(mbase[...] + far_part(other)).astype(BF16)
    message = layer_norm(dot(hidden, po_v[...])).astype(BF16)
    minflow = dot(minc[...], message).astype(BF16)
    hidden = silu(mself_term + dot(minflow, pin_v[...])).astype(BF16)
    update = layer_norm(dot(hidden, pf_v[...]))
    out_ref[0, 0] = (encoded.astype(F32) + update).astype(BF16)

    for copy, (*_, step) in zip(halo_copies, halo_moves):
        guarded(sends(step), copy.wait_send)
    for copy, (*_, step) in zip(near_copies, near_moves):
        guarded(sends(step), copy.wait_send)

    def end_row(k, carry):
        line_copy(k).wait_send()
        return carry

    lax.fori_loop(0, lat, end_row, 0)
    lax.fori_loop(lat + 1, nlat, end_row, 0)
    for turn, which in ((0, group), (1, other)):
        for k in range(1, nx):
            stage2(turn, which, k, first).wait_send()
            stage3(turn, which, k, second).wait_send()
        for k in range(nx):
            stage4(turn, which, core, k).wait_send()


def body(nx, ny, nlat, *args):
    weight = pltpu.VMEM((LATENT, LATENT), BF16)
    narrow = pltpu.VMEM((4, LATENT), BF16)
    half_line = nlat // 2
    sectors = nx * ny * half_line
    dma = pltpu.SemaphoreType.DMA
    scratch = [
        pltpu.VMEM((GRID_LAT, GRID_LON, LATENT), BF16), pltpu.VMEM((SLOTS, LATENT), BF16),
        pltpu.VMEM((1, GRID_EDGES), I32), pltpu.VMEM((1, GRID_EDGES), I32), pltpu.VMEM((4, GRID_EDGES), BF16),
        pltpu.VMEM((1, MESH_EDGES), I32), pltpu.VMEM((1, MESH_EDGES), I32), pltpu.VMEM((4, MESH_EDGES), BF16),
        pltpu.VMEM((1, 1, 2), I32),
        weight, weight, narrow, weight, weight, weight, weight,
        weight, weight, narrow, weight, weight, weight, weight,
        pltpu.VMEM((OWN, LATENT), BF16), pltpu.VMEM((PACKED, LATENT), BF16), pltpu.VMEM((HALO, LATENT), BF16),
        pltpu.VMEM((128, LATENT), BF16), pltpu.VMEM((GRID_EDGES, 8), F32), pltpu.VMEM((GRID_EDGES, HALO), BF16),
        pltpu.VMEM((GRID_EDGES, LATENT), F32), pltpu.VMEM((SLOTS, GRID_EDGES), BF16),
        pltpu.VMEM((512, LATENT), BF16),
        pltpu.VMEM((128, LATENT), BF16), pltpu.VMEM((MESH_EDGES, 8), F32), pltpu.VMEM((MESH_EDGES, 512), BF16),
        pltpu.VMEM((2, 2, MESH_EDGES, sectors), BF16),
        pltpu.VMEM((MESH_EDGES, LATENT), F32), pltpu.VMEM((SLOTS, MESH_EDGES), BF16),
        pltpu.VMEM((1, LATENT), F32), pltpu.VMEM((nlat, 1, LATENT), F32), pltpu.VMEM((2, 2, nx, nx, half_line, HALF), BF16),
        dma((23,)), pltpu.SemaphoreType.REGULAR, pltpu.SemaphoreType.REGULAR, dma((8,)), dma((8,)), dma((4,)), dma((4,)), dma((nlat,)), dma((nlat,)),
        dma((2, nx)), dma((2, nx)), dma((2, nx)), dma((2, nx)), dma((2, nx)), dma((2, nx)),
    ]
    return pl.pallas_call(
        functools.partial(kernel, nx, ny, nlat),
        out_shape=pltpu.VMEM((1, 1, SLOTS, LATENT), BF16),
        in_specs=[pl.BlockSpec(memory_space=pl.ANY)] * 23,
        out_specs=pl.BlockSpec(memory_space=pltpu.VMEM),
        scratch_shapes=scratch,
        compiler_params=pltpu.CompilerParams(collective_id=0, has_side_effects=True, vmem_limit_bytes=60 * 2**20),
        cost_estimate=pl.CostEstimate(flops=3 * 10**9, bytes_accessed=6 * 10**6, transcendentals=10**6),
    )(*args[:8], jnp.transpose(args[8], (1, 2, 0)), *args[9:])


def solution(mesh):
    nlon, nlat = mesh.shape["lon"], mesh.shape["lat"]
    nx = round(nlon**0.5)
    return jax.shard_map(
        functools.partial(body, nx, nlon // nx, nlat),
        mesh=mesh,
        in_specs=(
            P("lat", "lon", None),
            P("lat", "lon", None, None),
            P("lat", "lon", None),
            P("lat", "lon", None),
            P("lat", "lon", None, None),
            P("lat", "lon", None),
            P("lat", "lon", None),
            P("lat", "lon", None, None),
            P(None, "lat", "lon"),
        )
        + (P(),) * 14,
        out_specs=P("lat", "lon", None, None),
        check_vma=False,
    )
```

```python
import functools

import jax
import jax.numpy as jnp
from jax import lax
from jax.experimental import pallas as pl
from jax.experimental.pallas import tpu as pltpu
from jax.sharding import PartitionSpec as P

MESH = pl.DeviceIdType.MESH
LATENT = 512
HALF = 256
GRID_LAT = 16
GRID_LON = 32
RIM = 3
SLOTS = 40
BLOCK = 48
GRID_EDGES = 1024
MESH_EDGES = 512
TILE = 256
OWN = GRID_LAT * GRID_LON
UP, DOWN, LEFT, RIGHT = 0, 96, 192, 240
CORNER = 288
HALO = 384
PACKED = 160
GEO = 96
BF16, F32, I32 = jnp.bfloat16, jnp.float32, jnp.int32


def dot(a, b):
    return jnp.dot(a, b, preferred_element_type=F32)


def silu(v):
    half = 0.5 * v
    return half + half * jnp.tanh(half)


def layer_norm(v):
    centre = jnp.mean(v, axis=-1, keepdims=True)
    shifted = v - centre
    spread = jnp.mean(shifted * shifted, axis=-1, keepdims=True)
    return shifted * lax.rsqrt(spread + 1e-5)


def lanes(rows, columns):
    return lax.broadcasted_iota(I32, (rows, columns), 1).astype(F32)


def one_hot(column, width):
    return jnp.where(lanes(column.shape[0], width) == column, 1.0, 0.0).astype(BF16)


def target_hot(columns):
    place = lanes(columns.shape[0], 128)
    target = columns[:, 5:6]
    hot = jnp.where((place == target) | (place == target + BLOCK), 1.0, 0.0)
    for f in range(4):
        hot = jnp.where(place == GEO + f, columns[:, f : f + 1], hot)
    return hot.astype(BF16)


def fill_target_table(table, nodes, w_target, w_geometry):
    term = dot(nodes, w_target)
    high = term.astype(BF16)
    table[...] = jnp.zeros_like(table)
    table[0:SLOTS, :] = high
    table[BLOCK : BLOCK + SLOTS, :] = (term - high.astype(F32)).astype(BF16)
    table[GEO : GEO + 4, :] = w_geometry


def incidence(targets, count):
    edges = targets.shape[1]
    slot = lax.broadcasted_iota(I32, (SLOTS, edges), 0)
    live = lax.broadcasted_iota(I32, (SLOTS, edges), 1) < count
    return jnp.where((slot == targets) & live, 1.0, 0.0).astype(BF16)


def transposed(rows):
    return jnp.transpose(jnp.concatenate(rows, axis=0), (1, 0))


def kernel(nx, ny, nlat, *refs):
    (
        grid_hbm, mesh_hbm, gs_hbm, gt_hbm, gg_hbm, ms_hbm, mt_hbm, mg_hbm, ec_hbm,
        es_hbm, et_hbm, eg_hbm, eo_hbm, ei_hbm, ein_hbm, ef_hbm,
        ps_hbm, pt_hbm, pg_hbm, po_hbm, pi_hbm, pin_hbm, pf_hbm,
        out_ref,
        x_v, nodes_v, gs_v, gt_v, gg_v, ms_v, mt_v, mg_v, ec_v,
        es_v, et_v, eg_v, eo_v, ei_v, ein_v, ef_v,
        ps_v, pt_v, pg_v, po_v, pi_v, pin_v, pf_v,
        own_t, packed, up_v, down_v, side_v, halo_t, tg_t, columns_v, halo_hot, base, inc,
        near_t, mtg_t, mcolumns_v, near_hot, far_hot, mbase, minc,
        row_mine, rows_in, far_t,
        in_sem, late_mate, late_other, late_plane, halo_ss, halo_rs, near_ss, near_rs, s1_ss, s1_rs, s2_ss, s2_rs, s3_ss, s3_rs, s4_ss, s4_rs,
    ) = refs
    nlon, half_line = nx * ny, nlat // 2
    lon, lat = lax.axis_index("lon"), lax.axis_index("lat")
    core = lax.rem(lat, 2)
    x, y = lon // ny, lax.rem(lon, ny)
    first = jnp.where(core == 0, x, y)
    second = jnp.where(core == 0, y, x)
    first_step = jnp.where(core == 0, ny, 1)
    second_step = jnp.where(core == 0, 1, ny)
    group = lat // half_line
    other = 1 - group
    place_in_line = lax.rem(lat, half_line)
    has_above, has_below = lat > 0, lat < nlat - 1

    sources = [
        (grid_hbm, x_v), (es_hbm, es_v),
        (et_hbm, et_v), (eg_hbm, eg_v), (mesh_hbm.at[0, 0], nodes_v), (gs_hbm.at[0], gs_v), (gt_hbm.at[0], gt_v),
        (gg_hbm.at[0, 0], gg_v), (ec_hbm, ec_v), (eo_hbm, eo_v),
        (ei_hbm, ei_v), (ein_hbm, ein_v), (ef_hbm, ef_v), (ps_hbm, ps_v),
        (ms_hbm.at[0], ms_v), (mt_hbm.at[0], mt_v), (mg_hbm.at[0, 0], mg_v),
        (pt_hbm, pt_v), (pg_hbm, pg_v), (po_hbm, po_v), (pi_hbm, pi_v), (pin_hbm, pin_v), (pf_hbm, pf_v),
    ]
    loads = [pltpu.make_async_copy(src, dst, in_sem.at[k]) for k, (src, dst) in enumerate(sources)]
    loads[0].start()
    loads[1].start()

    around = [(0, 1), (0, -1), (1, 0), (-1, 0), (1, 1), (1, -1), (-1, 1), (-1, -1)]

    def neighbour(step):
        return (lax.rem(lon + step[1] + nlon, nlon), lat + step[0])

    def receives(step):
        return {0: None, 1: has_above, -1: has_below}[step[0]]

    def sends(step):
        return {0: None, 1: has_below, -1: has_above}[step[0]]

    def guarded(condition, act):
        if condition is None:
            act()
        else:
            pl.when(condition)(act)

    def first_peer(k):
        return (lax.rem(first + k, nx) * first_step + second * second_step, lat)

    def second_peer(k):
        return (first * first_step + lax.rem(second + k, nx) * second_step, lat)

    barrier = pltpu.get_barrier_semaphore()

    def greet(device):
        pl.semaphore_signal(barrier, inc=1, device_id=device, device_id_type=MESH)

    for step in around:
        if step[1] != 0:
            guarded(sends(step), functools.partial(greet, neighbour(step)))

    @pl.when(has_above)
    def _():
        greet((lon, lat - 1))

    def greet_line(k, carry):
        greet((lon, k))
        return carry

    def ranked(k):
        return jnp.where(k < nx // 2, k, nx + nx // 2 - 1 - k)

    def along_x(k):
        return (ranked(k) * ny + y, lat)

    def along_y(k):
        return (x * ny + ranked(k), lat)

    def greet_x(k, carry):
        greet(along_x(k))
        return carry

    def greet_y(k, carry):
        greet(along_y(k))
        return carry

    lax.fori_loop(lat + 1, nlat, greet_line, 0)
    lax.fori_loop(ranked(x) + 1, nx, greet_x, 0)
    lax.fori_loop(ranked(y) + 1, nx, greet_y, 0)
    greetings = 2 + 2 * jnp.where(has_above, 1, 0) + 3 * jnp.where(has_below, 1, 0) + lat + ranked(x) + ranked(y)

    place = lax.broadcasted_iota(I32, (PACKED, 128), 0)
    side = jnp.where(place < 48, place, place - 48)
    third = (side * 43) >> 7
    edge_row = third * GRID_LON + (side - 3 * third) + jnp.where(place < 48, GRID_LON - RIM, 0)
    corner = (place - 96) & 15
    which = (place - 96) >> 4
    third = (corner * 43) >> 7
    corner_row = (third + jnp.where(which < 2, GRID_LAT - RIM, 0)) * GRID_LON + (corner - 3 * third)
    corner_row = corner_row + jnp.where((which & 1) == 0, GRID_LON - RIM, 0)
    corner_row = jnp.where(corner < 9, corner_row, -1)
    wanted = jnp.where(place < 96, edge_row, corner_row)
    wanted = jnp.concatenate([wanted] * (OWN // 128), axis=1)
    pick = jnp.where(lax.broadcasted_iota(I32, (PACKED, OWN), 1) == wanted, 1.0, 0.0).astype(BF16)
    loads[0].wait()
    for load in loads[2:10]:
        load.start()
    packed[...] = dot(pick, x_v[...].reshape(OWN, LATENT)).astype(BF16)

    pl.semaphore_wait(barrier, greetings)

    halo_moves = [
        (packed.at[pl.ds(0, 48)], side_v.at[pl.ds(0, 48)], (0, 1)),
        (packed.at[pl.ds(48, 48)], side_v.at[pl.ds(48, 48)], (0, -1)),
        (x_v.at[pl.ds(GRID_LAT - RIM, RIM)], up_v, (1, 0)),
        (x_v.at[pl.ds(0, RIM)], down_v, (-1, 0)),
        (packed.at[pl.ds(96, 16)], side_v.at[pl.ds(96, 16)], (1, 1)),
        (packed.at[pl.ds(112, 16)], side_v.at[pl.ds(112, 16)], (1, -1)),
        (packed.at[pl.ds(128, 16)], side_v.at[pl.ds(128, 16)], (-1, 1)),
        (packed.at[pl.ds(144, 16)], side_v.at[pl.ds(144, 16)], (-1, -1)),
    ]
    halo_copies = [
        pltpu.make_async_remote_copy(
            src_ref=src, dst_ref=dst, send_sem=halo_ss.at[k], recv_sem=halo_rs.at[k],
            device_id=neighbour(step), device_id_type=MESH,
        )
        for k, (src, dst, step) in enumerate(halo_moves)
    ]
    for copy, (*_, step) in zip(halo_copies, halo_moves):
        guarded(sends(step), copy.start)

    for load in loads[10:]:
        load.start()

    def report_mate(k, carry):
        pl.semaphore_signal(late_mate, inc=1, device_id=(lon, k), device_id_type=MESH)
        return carry

    def report_other(k, carry):
        pl.semaphore_signal(late_other, inc=1, device_id=(lon, k), device_id_type=MESH)
        return carry

    def report_x(k, carry):
        pl.semaphore_signal(late_plane, inc=1, device_id=along_x(k), device_id_type=MESH)
        return carry

    def report_y(k, carry):
        pl.semaphore_signal(late_plane, inc=1, device_id=along_y(k), device_id_type=MESH)
        return carry

    lax.fori_loop(0, ranked(x), report_x, 0)
    lax.fori_loop(0, ranked(y), report_y, 0)
    lax.fori_loop(group * half_line, lat, report_mate, 0)
    lax.fori_loop(0, group * half_line, report_other, 0)

    side_v[pl.ds(PACKED, 32), :] = jnp.zeros((32, LATENT), BF16)

    @pl.when(lat == 0)
    def _():
        up_v[...] = jnp.zeros_like(up_v)
        side_v[pl.ds(96, 32), :] = jnp.zeros((32, LATENT), BF16)
        near_t[pl.ds(0, 3 * BLOCK), :] = jnp.zeros((3 * BLOCK, LATENT), BF16)

    @pl.when(lat == nlat - 1)
    def _():
        down_v[...] = jnp.zeros_like(down_v)
        side_v[pl.ds(128, 32), :] = jnp.zeros((32, LATENT), BF16)
        near_t[pl.ds(6 * BLOCK, 3 * BLOCK), :] = jnp.zeros((3 * BLOCK, LATENT), BF16)

    loads[1].wait()
    own_t[...] = dot(x_v[...].reshape(OWN, LATENT), es_v[...]).astype(BF16)

    for load in loads[2:10]:
        load.wait()
    nodes = nodes_v[...]
    fill_target_table(tg_t, nodes, et_v[...], eg_v[...])
    s = gs_v[...]
    r = (s * 1725) >> 16
    c = s - r * (GRID_LON + 2 * RIM)
    above, below = r < RIM, r >= GRID_LAT + RIM
    before, after = c < RIM, c >= GRID_LON + RIM
    row_in = jnp.where(above, r, jnp.where(below, r - GRID_LAT - RIM, r - RIM))
    col_in = jnp.where(before, c, jnp.where(after, c - GRID_LON - RIM, c - RIM))
    beside, over = before | after, above | below
    wide = row_in * GRID_LON + col_in
    thin = row_in * RIM + col_in
    own_at = jnp.where(beside | over, -1, wide)
    over_at = wide + jnp.where(above, UP, DOWN)
    beside_at = thin + jnp.where(before, LEFT, RIGHT)
    corner_at = thin + CORNER + jnp.where(above, 0, 32) + jnp.where(before, 0, 16)
    halo_at = jnp.where(over, jnp.where(beside, corner_at, over_at), jnp.where(beside, beside_at, -1))
    targets = gt_v[...]
    columns_v[...] = transposed([
        gg_v[...].astype(F32), own_at.astype(F32), targets.astype(F32), halo_at.astype(F32),
        jnp.zeros((1, GRID_EDGES), F32),
    ])
    inc[...] = incidence(targets, ec_v[0, :, 0:1])

    def grid_base(i, carry):
        edges = pl.ds(pl.multiple_of(i * TILE, TILE), TILE)
        columns = columns_v[edges, :]
        total = dot(one_hot(columns[:, 4:5], OWN), own_t[...])
        base[edges, :] = total + dot(target_hot(columns), tg_t[...])
        halo_hot[edges, :] = one_hot(columns[:, 6:7], HALO)
        return carry

    lax.fori_loop(0, GRID_EDGES // TILE, grid_base, 0, unroll=True)
    for load in loads[10:14]:
        load.wait()
    self_term = dot(nodes, ei_v[...])

    for copy, (*_, step) in zip(halo_copies, halo_moves):
        guarded(receives(step), copy.wait_recv)

    halo_t[0:96, :] = dot(up_v[...].reshape(96, LATENT), es_v[...]).astype(BF16)
    halo_t[96:192, :] = dot(down_v[...].reshape(96, LATENT), es_v[...]).astype(BF16)
    halo_t[192:HALO, :] = dot(side_v[...], es_v[...]).astype(BF16)
    hidden = silu(base[...] + dot(halo_hot[...], halo_t[...])).astype(BF16)
    message = layer_norm(dot(hidden, eo_v[...])).astype(BF16)
    inflow = dot(inc[...], message).astype(BF16)
    hidden = silu(self_term + dot(inflow, ein_v[...])).astype(BF16)
    encoded = (nodes.astype(F32) + layer_norm(dot(hidden, ef_v[...]))).astype(BF16)
    term = dot(encoded, ps_v[...]).astype(BF16)

    row_mine[...] = term.astype(F32)[0:1, :]
    rows_in[lat] = term.astype(F32)[0:1, :]

    def line_copy(target):
        return pltpu.make_async_remote_copy(
            src_ref=row_mine, dst_ref=rows_in.at[lat], send_sem=s1_ss.at[target], recv_sem=s1_rs.at[lat],
            device_id=(lon, target), device_id_type=MESH,
        )

    def line_arrival(source):
        return pltpu.make_async_remote_copy(
            src_ref=row_mine, dst_ref=rows_in.at[source], send_sem=s1_ss.at[source], recv_sem=s1_rs.at[source],
            device_id=(lon, source), device_id_type=MESH,
        )

    def send_row(k, carry):
        line_copy(k).start()
        return carry

    lax.fori_loop(0, lat, send_row, 0)

    @pl.when(place_in_line < half_line - 1)
    def _():
        pl.semaphore_wait(late_mate, half_line - 1 - place_in_line)

    lax.fori_loop(lat + 1, (group + 1) * half_line, send_row, 0)

    near_t[pl.ds(4 * BLOCK, SLOTS), :] = term
    near_t[pl.ds(4 * BLOCK + SLOTS, BLOCK - SLOTS), :] = jnp.zeros((BLOCK - SLOTS, LATENT), BF16)
    near_t[pl.ds(9 * BLOCK, 512 - 9 * BLOCK), :] = jnp.zeros((512 - 9 * BLOCK, LATENT), BF16)
    near_moves = [(4, 3, 1, (0, 1)), (4, 5, 1, (0, -1)), (3, 0, 3, (1, 0)), (3, 6, 3, (-1, 0))]
    near_copies = [
        pltpu.make_async_remote_copy(
            src_ref=near_t.at[pl.ds(source * BLOCK, blocks * BLOCK)], dst_ref=near_t.at[pl.ds(at * BLOCK, blocks * BLOCK)],
            send_sem=near_ss.at[k], recv_sem=near_rs.at[k], device_id=neighbour(step), device_id_type=MESH,
        )
        for k, (source, at, blocks, step) in enumerate(near_moves)
    ]
    near_copies[0].start()
    near_copies[1].start()

    for load in loads[14:23]:
        load.wait()
    fill_target_table(mtg_t, encoded, pt_v[...], pg_v[...])
    s = ms_v[...]
    sectors = nlon * half_line

    def slot_of(step):
        step = jnp.where(step < 0, step + nx, step)
        return jnp.where(step == 0, 0, jnp.where(step <= nx // 2, 2 * step - 1, 2 * (nx - step)))

    near = s < 9 * SLOTS
    sector = (s * 1639) >> 16
    near_at = jnp.where(near, sector * BLOCK + (s - sector * SLOTS), -1)
    t = s - 9 * SLOTS
    plane, line = t // nlat, lax.rem(t, nlat)
    far_x, far_y = plane // ny, lax.rem(plane, ny)
    offset = (line // half_line) * sectors + lax.rem(line, half_line)
    far_at0 = jnp.where(near, -1, (far_y * nx + slot_of(far_x - x)) * half_line + offset)
    far_at1 = jnp.where(near, -1, (far_x * nx + slot_of(far_y - y)) * half_line + offset)
    targets = mt_v[...]
    mcolumns_v[...] = transposed([
        mg_v[...].astype(F32), near_at.astype(F32), targets.astype(F32), far_at0.astype(F32), far_at1.astype(F32),
    ])
    minc[...] = incidence(targets, ec_v[0, :, 1:2])

    columns = mcolumns_v[...]
    near_hot[...] = one_hot(columns[:, 4:5], 512)
    mbase[...] = dot(target_hot(columns), mtg_t[...])
    for g in range(2):
        far_hot[0, g] = one_hot(columns[:, 6:7] - g * sectors, sectors)
        far_hot[1, g] = one_hot(columns[:, 7:8] - g * sectors, sectors)
    mself_term = dot(encoded, pi_v[...])

    near_copies[0].wait_recv()
    near_copies[1].wait_recv()
    for k in (2, 3):
        guarded(sends(near_moves[k][3]), near_copies[k].start)

    def place_rows(which):
        row_at = lax.broadcasted_iota(I32, (half_line, LATENT), 0)
        block = jnp.zeros((half_line, LATENT), F32)
        for k in range(half_line):
            block = jnp.where(row_at == k, rows_in[which * half_line + k], block)
        half = jnp.where(core == 0, block[:, :HALF], block[:, HALF:])
        far_t[which, core, second, 0] = half.astype(BF16)

    def fixed_slot(step):
        return 0 if step == 0 else 2 * step - 1 if step <= nx // 2 else 2 * (nx - step)

    def stage2(turn, which, k):
        slot = fixed_slot(nx - k)
        return pltpu.make_async_remote_copy(
            src_ref=far_t.at[which, core, second, 0], dst_ref=far_t.at[which, core, second, slot],
            send_sem=s2_ss.at[turn, slot], recv_sem=s2_rs.at[turn, slot], device_id=first_peer(k), device_id_type=MESH,
        )

    parts = [(0, 3), (3, 5), (5, 7), (7, 8)] if nx == 8 else [(0, 1), (1, nx)]

    def stage3(turn, which, part, k, source):
        low, high = parts[part]
        at = far_t.at[which, core, source, pl.ds(low, high - low)]
        return pltpu.make_async_remote_copy(
            src_ref=at, dst_ref=at, send_sem=s3_ss.at[turn, part, k], recv_sem=s3_rs.at[turn, part, source],
            device_id=second_peer(k), device_id_type=MESH,
        )

    def stage4(turn, which, half_of, source):
        at = far_t.at[which, half_of, source]
        return pltpu.make_async_remote_copy(
            src_ref=at, dst_ref=at, send_sem=s4_ss.at[turn, source], recv_sem=s4_rs.at[turn, source],
            device_id=(lon, lat + 1 - 2 * core), device_id_type=MESH,
        )

    order = sorted(range(1, nx), key=lambda k: min(k, nx - k))

    def start2(turn, which):
        for k in range(1, nx):
            stage2(turn, which, k).start()

    def start3(turn, which):
        for part, (low, high) in enumerate(parts):
            for k in range(1, nx):
                if low <= fixed_slot(nx - k) < high:
                    stage2(turn, which, k).wait_recv()
            for k in reversed(order):
                stage3(turn, which, part, k, second).start()
        stage4(turn, which, core, second).start()

    def hand_on(turn, which):
        for k in order:
            source = lax.rem(second + k, nx)
            for part in range(len(parts)):
                stage3(turn, which, part, k, source).wait_recv()
            stage4(turn, which, core, source).start()

    def wait4(turn, which):
        for k in range(nx):
            stage4(turn, which, 1 - core, k).wait_recv()

    def far_part(which):
        parts = [dot(far_hot[h, which], far_t[which, h].reshape(sectors, HALF)) for h in range(2)]
        return jnp.concatenate(parts, axis=1)

    def wait_row(k, carry):
        line_arrival(k).wait_recv()
        return carry

    lax.fori_loop(group * half_line, lat, wait_row, 0)
    lax.fori_loop(lat + 1, (group + 1) * half_line, wait_row, 0)
    place_rows(group)
    later = 2 * (nx - 1) - ranked(x) - ranked(y)

    @pl.when(later > 0)
    def _():
        pl.semaphore_wait(late_plane, later)

    start2(0, group)

    @pl.when(group == 0)
    def _():
        pl.semaphore_wait(late_other, half_line)
        lax.fori_loop(half_line, nlat, send_row, 0)

    lax.fori_loop(other * half_line, (other + 1) * half_line, wait_row, 0)
    place_rows(other)
    start2(1, other)
    start3(0, group)
    for k in (2, 3):
        guarded(receives(near_moves[k][3]), near_copies[k].wait_recv)
    mbase[...] += dot(near_hot[...], near_t[...])
    start3(1, other)
    hand_on(0, group)
    wait4(0, group)
    mbase[...] += far_part(group)
    hand_on(1, other)
    wait4(1, other)
    hidden = silu(mbase[...] + far_part(other)).astype(BF16)
    message = layer_norm(dot(hidden, po_v[...])).astype(BF16)
    minflow = dot(minc[...], message).astype(BF16)
    hidden = silu(mself_term + dot(minflow, pin_v[...])).astype(BF16)
    update = layer_norm(dot(hidden, pf_v[...]))
    out_ref[0, 0] = (encoded.astype(F32) + update).astype(BF16)

    for copy, (*_, step) in zip(halo_copies, halo_moves):
        guarded(sends(step), copy.wait_send)
    for copy, (*_, step) in zip(near_copies, near_moves):
        guarded(sends(step), copy.wait_send)

    def end_row(k, carry):
        line_copy(k).wait_send()
        return carry

    lax.fori_loop(0, lat, end_row, 0)
    lax.fori_loop(lat + 1, nlat, end_row, 0)
    for turn, which in ((0, group), (1, other)):
        for k in range(1, nx):
            stage2(turn, which, k).wait_send()
            for part in range(len(parts)):
                stage3(turn, which, part, k, second).wait_send()
        for k in range(nx):
            stage4(turn, which, core, k).wait_send()


def body(nx, ny, nlat, *args):
    weight = pltpu.VMEM((LATENT, LATENT), BF16)
    narrow = pltpu.VMEM((4, LATENT), BF16)
    half_line = nlat // 2
    sectors = nx * ny * half_line
    dma = pltpu.SemaphoreType.DMA
    scratch = [
        pltpu.VMEM((GRID_LAT, GRID_LON, LATENT), BF16), pltpu.VMEM((SLOTS, LATENT), BF16),
        pltpu.VMEM((1, GRID_EDGES), I32), pltpu.VMEM((1, GRID_EDGES), I32), pltpu.VMEM((4, GRID_EDGES), BF16),
        pltpu.VMEM((1, MESH_EDGES), I32), pltpu.VMEM((1, MESH_EDGES), I32), pltpu.VMEM((4, MESH_EDGES), BF16),
        pltpu.VMEM((1, 1, 2), I32),
        weight, weight, narrow, weight, weight, weight, weight,
        weight, weight, narrow, weight, weight, weight, weight,
        pltpu.VMEM((OWN, LATENT), BF16), pltpu.VMEM((PACKED, LATENT), BF16), pltpu.VMEM((RIM, GRID_LON, LATENT), BF16),
        pltpu.VMEM((RIM, GRID_LON, LATENT), BF16), pltpu.VMEM((PACKED + 32, LATENT), BF16), pltpu.VMEM((HALO, LATENT), BF16),
        pltpu.VMEM((128, LATENT), BF16), pltpu.VMEM((GRID_EDGES, 8), F32), pltpu.VMEM((GRID_EDGES, HALO), BF16),
        pltpu.VMEM((GRID_EDGES, LATENT), F32), pltpu.VMEM((SLOTS, GRID_EDGES), BF16),
        pltpu.VMEM((512, LATENT), BF16),
        pltpu.VMEM((128, LATENT), BF16), pltpu.VMEM((MESH_EDGES, 8), F32), pltpu.VMEM((MESH_EDGES, 512), BF16),
        pltpu.VMEM((2, 2, MESH_EDGES, sectors), BF16),
        pltpu.VMEM((MESH_EDGES, LATENT), F32), pltpu.VMEM((SLOTS, MESH_EDGES), BF16),
        pltpu.VMEM((1, LATENT), F32), pltpu.VMEM((nlat, 1, LATENT), F32), pltpu.VMEM((2, 2, nx, nx, half_line, HALF), BF16),
        dma((23,)), pltpu.SemaphoreType.REGULAR, pltpu.SemaphoreType.REGULAR, pltpu.SemaphoreType.REGULAR, dma((8,)), dma((8,)), dma((4,)), dma((4,)), dma((nlat,)), dma((nlat,)),
        dma((2, nx)), dma((2, nx)), dma((2, 4, nx)), dma((2, 4, nx)), dma((2, nx)), dma((2, nx)),
    ]
    return pl.pallas_call(
        functools.partial(kernel, nx, ny, nlat),
        out_shape=pltpu.VMEM((1, 1, SLOTS, LATENT), BF16),
        in_specs=[pl.BlockSpec(memory_space=pl.ANY)] * 23,
        out_specs=pl.BlockSpec(memory_space=pltpu.VMEM),
        scratch_shapes=scratch,
        compiler_params=pltpu.CompilerParams(collective_id=0, has_side_effects=True, vmem_limit_bytes=60 * 2**20),
        cost_estimate=pl.CostEstimate(flops=3 * 10**9, bytes_accessed=6 * 10**6, transcendentals=10**6),
    )(*args[:8], jnp.transpose(args[8], (1, 2, 0)), *args[9:])


def solution(mesh):
    nlon, nlat = mesh.shape["lon"], mesh.shape["lat"]
    nx = round(nlon**0.5)
    return jax.shard_map(
        functools.partial(body, nx, nlon // nx, nlat),
        mesh=mesh,
        in_specs=(
            P("lat", "lon", None),
            P("lat", "lon", None, None),
            P("lat", "lon", None),
            P("lat", "lon", None),
            P("lat", "lon", None, None),
            P("lat", "lon", None),
            P("lat", "lon", None),
            P("lat", "lon", None, None),
            P(None, "lat", "lon"),
        )
        + (P(),) * 14,
        out_specs=P("lat", "lon", None, None),
        check_vma=False,
    )
```

```python
import functools

import jax
import jax.numpy as jnp
from jax import lax
from jax.experimental import pallas as pl
from jax.experimental.pallas import tpu as pltpu
from jax.sharding import PartitionSpec as P

MESH = pl.DeviceIdType.MESH
LATENT = 512
HALF = 256
GRID_LAT = 16
GRID_LON = 32
RIM = 3
SLOTS = 40
BLOCK = 48
GRID_EDGES = 1024
MESH_EDGES = 512
TILE = 256
OWN = GRID_LAT * GRID_LON
UP, DOWN, LEFT, RIGHT = 0, 96, 192, 240
CORNER = 288
HALO = 384
PACKED = 160
GEO = 96
BF16, F32, I32 = jnp.bfloat16, jnp.float32, jnp.int32


def dot(a, b):
    return jnp.dot(a, b, preferred_element_type=F32)


def silu(v):
    half = 0.5 * v
    return half + half * jnp.tanh(half)


def layer_norm(v):
    centre = jnp.mean(v, axis=-1, keepdims=True)
    shifted = v - centre
    spread = jnp.mean(shifted * shifted, axis=-1, keepdims=True)
    return shifted * lax.rsqrt(spread + 1e-5)


def lanes(rows, columns):
    return lax.broadcasted_iota(I32, (rows, columns), 1).astype(F32)


def one_hot(column, width):
    return jnp.where(lanes(column.shape[0], width) == column, 1.0, 0.0).astype(BF16)


def target_hot(columns):
    place = lanes(columns.shape[0], 128)
    target = columns[:, 5:6]
    hot = jnp.where((place == target) | (place == target + BLOCK), 1.0, 0.0)
    for f in range(4):
        hot = jnp.where(place == GEO + f, columns[:, f : f + 1], hot)
    return hot.astype(BF16)


def fill_target_table(table, nodes, w_target, w_geometry):
    term = dot(nodes, w_target)
    high = term.astype(BF16)
    table[...] = jnp.zeros_like(table)
    table[0:SLOTS, :] = high
    table[BLOCK : BLOCK + SLOTS, :] = (term - high.astype(F32)).astype(BF16)
    table[GEO : GEO + 4, :] = w_geometry


def incidence(targets, count):
    edges = targets.shape[1]
    slot = lax.broadcasted_iota(I32, (SLOTS, edges), 0)
    live = lax.broadcasted_iota(I32, (SLOTS, edges), 1) < count
    return jnp.where((slot == targets) & live, 1.0, 0.0).astype(BF16)


def transposed(rows):
    return jnp.transpose(jnp.concatenate(rows, axis=0), (1, 0))


def kernel(nx, ny, nlat, *refs):
    (
        grid_hbm, mesh_hbm, gs_hbm, gt_hbm, gg_hbm, ms_hbm, mt_hbm, mg_hbm, ec_hbm,
        es_hbm, et_hbm, eg_hbm, eo_hbm, ei_hbm, ein_hbm, ef_hbm,
        ps_hbm, pt_hbm, pg_hbm, po_hbm, pi_hbm, pin_hbm, pf_hbm,
        out_ref,
        x_v, nodes_v, gs_v, gt_v, gg_v, ms_v, mt_v, mg_v, ec_v,
        es_v, et_v, eg_v, eo_v, ei_v, ein_v, ef_v,
        ps_v, pt_v, pg_v, po_v, pi_v, pin_v, pf_v,
        own_t, packed, up_v, down_v, side_v, halo_t, tg_t, columns_v, halo_hot, base, inc,
        near_t, mtg_t, mcolumns_v, near_hot, far_hot, mbase, minc,
        row_mine, rows_in, far_t,
        in_sem, late_mate, late_other, late_plane, halo_ss, halo_rs, near_ss, near_rs, s1_ss, s1_rs, s2_ss, s2_rs, s3_ss, s3_rs, s4_ss, s4_rs,
    ) = refs
    nlon, half_line = nx * ny, nlat // 2
    lon, lat = lax.axis_index("lon"), lax.axis_index("lat")
    core = lax.rem(lat, 2)
    x, y = lon // ny, lax.rem(lon, ny)
    first = jnp.where(core == 0, x, y)
    second = jnp.where(core == 0, y, x)
    first_step = jnp.where(core == 0, ny, 1)
    second_step = jnp.where(core == 0, 1, ny)
    group = lat // half_line
    other = 1 - group
    place_in_line = lax.rem(lat, half_line)
    has_above, has_below = lat > 0, lat < nlat - 1

    sources = [
        (grid_hbm, x_v), (es_hbm, es_v),
        (et_hbm, et_v), (eg_hbm, eg_v), (mesh_hbm.at[0, 0], nodes_v), (gs_hbm.at[0], gs_v), (gt_hbm.at[0], gt_v),
        (gg_hbm.at[0, 0], gg_v), (ec_hbm, ec_v), (eo_hbm, eo_v),
        (ei_hbm, ei_v), (ein_hbm, ein_v), (ef_hbm, ef_v), (ps_hbm, ps_v),
        (ms_hbm.at[0], ms_v), (mt_hbm.at[0], mt_v), (mg_hbm.at[0, 0], mg_v),
        (pt_hbm, pt_v), (pg_hbm, pg_v), (po_hbm, po_v), (pi_hbm, pi_v), (pin_hbm, pin_v), (pf_hbm, pf_v),
    ]
    loads = [pltpu.make_async_copy(src, dst, in_sem.at[k]) for k, (src, dst) in enumerate(sources)]
    loads[0].start()
    loads[1].start()

    around = [(0, 1), (0, -1), (1, 0), (-1, 0), (1, 1), (1, -1), (-1, 1), (-1, -1)]

    def neighbour(step):
        return (lax.rem(lon + step[1] + nlon, nlon), lax.rem(lat + step[0] + nlat, nlat))

    def receives(step):
        return {0: None, 1: has_above, -1: has_below}[step[0]]

    def sends(step):
        return {0: None, 1: has_below, -1: has_above}[step[0]]

    def guarded(condition, act):
        if condition is None:
            act()
        else:
            pl.when(condition)(act)

    def first_peer(k):
        return (lax.rem(first + k, nx) * first_step + second * second_step, lat)

    def second_peer(k):
        return (first * first_step + lax.rem(second + k, nx) * second_step, lat)

    barrier = pltpu.get_barrier_semaphore()

    def greet(device):
        pl.semaphore_signal(barrier, inc=1, device_id=device, device_id_type=MESH)

    for step in around:
        if step[1] != 0:
            guarded(sends(step), functools.partial(greet, neighbour(step)))

    @pl.when(has_above)
    def _():
        greet((lon, lat - 1))

    def greet_line(k, carry):
        greet((lon, k))
        return carry

    def ranked(k):
        return jnp.where(k < nx // 2, k, nx + nx // 2 - 1 - k)

    def along_x(k):
        return (ranked(k) * ny + y, lat)

    def along_y(k):
        return (x * ny + ranked(k), lat)

    def greet_x(k, carry):
        greet(along_x(k))
        return carry

    def greet_y(k, carry):
        greet(along_y(k))
        return carry

    lax.fori_loop(lat + 1, nlat, greet_line, 0)
    lax.fori_loop(ranked(x) + 1, nx, greet_x, 0)
    lax.fori_loop(ranked(y) + 1, nx, greet_y, 0)
    greetings = 2 + 2 * jnp.where(has_above, 1, 0) + 3 * jnp.where(has_below, 1, 0) + lat + ranked(x) + ranked(y)

    place = lax.broadcasted_iota(I32, (PACKED, 128), 0)
    side = jnp.where(place < 48, place, place - 48)
    third = (side * 43) >> 7
    edge_row = third * GRID_LON + (side - 3 * third) + jnp.where(place < 48, GRID_LON - RIM, 0)
    corner = (place - 96) & 15
    which = (place - 96) >> 4
    third = (corner * 43) >> 7
    corner_row = (third + jnp.where(which < 2, GRID_LAT - RIM, 0)) * GRID_LON + (corner - 3 * third)
    corner_row = corner_row + jnp.where((which & 1) == 0, GRID_LON - RIM, 0)
    corner_row = jnp.where(corner < 9, corner_row, -1)
    wanted = jnp.where(place < 96, edge_row, corner_row)
    wanted = jnp.concatenate([wanted] * (OWN // 128), axis=1)
    pick = jnp.where(lax.broadcasted_iota(I32, (PACKED, OWN), 1) == wanted, 1.0, 0.0).astype(BF16)
    loads[0].wait()
    for load in loads[2:10]:
        load.start()
    packed[...] = dot(pick, x_v[...].reshape(OWN, LATENT)).astype(BF16)

    pl.semaphore_wait(barrier, greetings)

    halo_moves = [
        (packed.at[pl.ds(0, 48)], side_v.at[pl.ds(0, 48)], (0, 1)),
        (packed.at[pl.ds(48, 48)], side_v.at[pl.ds(48, 48)], (0, -1)),
        (x_v.at[pl.ds(GRID_LAT - RIM, RIM)], up_v, (1, 0)),
        (x_v.at[pl.ds(0, RIM)], down_v, (-1, 0)),
        (packed.at[pl.ds(96, 16)], side_v.at[pl.ds(96, 16)], (1, 1)),
        (packed.at[pl.ds(112, 16)], side_v.at[pl.ds(112, 16)], (1, -1)),
        (packed.at[pl.ds(128, 16)], side_v.at[pl.ds(128, 16)], (-1, 1)),
        (packed.at[pl.ds(144, 16)], side_v.at[pl.ds(144, 16)], (-1, -1)),
    ]
    halo_copies = [
        pltpu.make_async_remote_copy(
            src_ref=src, dst_ref=dst, send_sem=halo_ss.at[k], recv_sem=halo_rs.at[k],
            device_id=neighbour(step), device_id_type=MESH,
        )
        for k, (src, dst, step) in enumerate(halo_moves)
    ]
    for copy, (*_, step) in zip(halo_copies, halo_moves):
        guarded(sends(step), copy.start)

    for load in loads[10:]:
        load.start()

    def report_mate(k, carry):
        pl.semaphore_signal(late_mate, inc=1, device_id=(lon, k), device_id_type=MESH)
        return carry

    def report_other(k, carry):
        pl.semaphore_signal(late_other, inc=1, device_id=(lon, k), device_id_type=MESH)
        return carry

    def report_x(k, carry):
        pl.semaphore_signal(late_plane, inc=1, device_id=along_x(k), device_id_type=MESH)
        return carry

    def report_y(k, carry):
        pl.semaphore_signal(late_plane, inc=1, device_id=along_y(k), device_id_type=MESH)
        return carry

    lax.fori_loop(0, ranked(x), report_x, 0)
    lax.fori_loop(0, ranked(y), report_y, 0)
    lax.fori_loop(group * half_line, lat, report_mate, 0)
    lax.fori_loop(0, group * half_line, report_other, 0)

    side_v[pl.ds(PACKED, 32), :] = jnp.zeros((32, LATENT), BF16)

    @pl.when(lat == 0)
    def _():
        up_v[...] = jnp.zeros_like(up_v)
        side_v[pl.ds(96, 32), :] = jnp.zeros((32, LATENT), BF16)
        near_t[pl.ds(0, 3 * BLOCK), :] = jnp.zeros((3 * BLOCK, LATENT), BF16)

    @pl.when(lat == nlat - 1)
    def _():
        down_v[...] = jnp.zeros_like(down_v)
        side_v[pl.ds(128, 32), :] = jnp.zeros((32, LATENT), BF16)
        near_t[pl.ds(6 * BLOCK, 3 * BLOCK), :] = jnp.zeros((3 * BLOCK, LATENT), BF16)

    loads[1].wait()
    own_t[...] = dot(x_v[...].reshape(OWN, LATENT), es_v[...]).astype(BF16)

    for load in loads[2:10]:
        load.wait()
    nodes = nodes_v[...]
    fill_target_table(tg_t, nodes, et_v[...], eg_v[...])
    s = gs_v[...]
    r = (s * 1725) >> 16
    c = s - r * (GRID_LON + 2 * RIM)
    above, below = r < RIM, r >= GRID_LAT + RIM
    before, after = c < RIM, c >= GRID_LON + RIM
    row_in = jnp.where(above, r, jnp.where(below, r - GRID_LAT - RIM, r - RIM))
    col_in = jnp.where(before, c, jnp.where(after, c - GRID_LON - RIM, c - RIM))
    beside, over = before | after, above | below
    wide = row_in * GRID_LON + col_in
    thin = row_in * RIM + col_in
    own_at = jnp.where(beside | over, -1, wide)
    over_at = wide + jnp.where(above, UP, DOWN)
    beside_at = thin + jnp.where(before, LEFT, RIGHT)
    corner_at = thin + CORNER + jnp.where(above, 0, 32) + jnp.where(before, 0, 16)
    halo_at = jnp.where(over, jnp.where(beside, corner_at, over_at), jnp.where(beside, beside_at, -1))
    targets = gt_v[...]
    columns_v[...] = transposed([
        gg_v[...].astype(F32), own_at.astype(F32), targets.astype(F32), halo_at.astype(F32),
        jnp.zeros((1, GRID_EDGES), F32),
    ])
    inc[...] = incidence(targets, ec_v[0, :, 0:1])

    def grid_base(i, carry):
        edges = pl.ds(pl.multiple_of(i * TILE, TILE), TILE)
        columns = columns_v[edges, :]
        total = dot(one_hot(columns[:, 4:5], OWN), own_t[...])
        base[edges, :] = total + dot(target_hot(columns), tg_t[...])
        halo_hot[edges, :] = one_hot(columns[:, 6:7], HALO)
        return carry

    lax.fori_loop(0, GRID_EDGES // TILE, grid_base, 0, unroll=True)
    for load in loads[10:14]:
        load.wait()
    self_term = dot(nodes, ei_v[...])

    for copy, (*_, step) in zip(halo_copies, halo_moves):
        guarded(receives(step), copy.wait_recv)

    halo_t[0:96, :] = dot(up_v[...].reshape(96, LATENT), es_v[...]).astype(BF16)
    halo_t[96:192, :] = dot(down_v[...].reshape(96, LATENT), es_v[...]).astype(BF16)
    halo_t[192:HALO, :] = dot(side_v[...], es_v[...]).astype(BF16)
    hidden = silu(base[...] + dot(halo_hot[...], halo_t[...])).astype(BF16)
    message = layer_norm(dot(hidden, eo_v[...])).astype(BF16)
    inflow = dot(inc[...], message).astype(BF16)
    hidden = silu(self_term + dot(inflow, ein_v[...])).astype(BF16)
    encoded = (nodes.astype(F32) + layer_norm(dot(hidden, ef_v[...]))).astype(BF16)
    term = dot(encoded, ps_v[...]).astype(BF16)

    row_mine[...] = term.astype(F32)[0:1, :]
    rows_in[lat] = term.astype(F32)[0:1, :]

    def line_copy(target):
        return pltpu.make_async_remote_copy(
            src_ref=row_mine, dst_ref=rows_in.at[lat], send_sem=s1_ss.at[target], recv_sem=s1_rs.at[lat],
            device_id=(lon, target), device_id_type=MESH,
        )

    def line_arrival(source):
        return pltpu.make_async_remote_copy(
            src_ref=row_mine, dst_ref=rows_in.at[source], send_sem=s1_ss.at[source], recv_sem=s1_rs.at[source],
            device_id=(lon, source), device_id_type=MESH,
        )

    def send_row(k, carry):
        line_copy(k).start()
        return carry

    lax.fori_loop(0, lat, send_row, 0)

    @pl.when(place_in_line < half_line - 1)
    def _():
        pl.semaphore_wait(late_mate, half_line - 1 - place_in_line)

    lax.fori_loop(lat + 1, (group + 1) * half_line, send_row, 0)

    near_t[pl.ds(4 * BLOCK, SLOTS), :] = term
    near_t[pl.ds(4 * BLOCK + SLOTS, BLOCK - SLOTS), :] = jnp.zeros((BLOCK - SLOTS, LATENT), BF16)
    near_t[pl.ds(9 * BLOCK, 512 - 9 * BLOCK), :] = jnp.zeros((512 - 9 * BLOCK, LATENT), BF16)
    near_moves = [(4, 3, 1, (0, 1)), (4, 5, 1, (0, -1)), (3, 0, 3, (1, 0)), (3, 6, 3, (-1, 0))]
    near_copies = [
        pltpu.make_async_remote_copy(
            src_ref=near_t.at[pl.ds(source * BLOCK, blocks * BLOCK)], dst_ref=near_t.at[pl.ds(at * BLOCK, blocks * BLOCK)],
            send_sem=near_ss.at[k], recv_sem=near_rs.at[k], device_id=neighbour(step), device_id_type=MESH,
        )
        for k, (source, at, blocks, step) in enumerate(near_moves)
    ]
    near_copies[0].start()
    near_copies[1].start()

    for load in loads[14:23]:
        load.wait()
    fill_target_table(mtg_t, encoded, pt_v[...], pg_v[...])
    s = ms_v[...]
    sectors = nlon * half_line

    def slot_of(step):
        step = jnp.where(step < 0, step + nx, step)
        return jnp.where(step == 0, 0, jnp.where(step <= nx // 2, 2 * step - 1, 2 * (nx - step)))

    near = s < 9 * SLOTS
    sector = (s * 1639) >> 16
    near_at = jnp.where(near, sector * BLOCK + (s - sector * SLOTS), -1)
    t = s - 9 * SLOTS
    plane, line = t // nlat, lax.rem(t, nlat)
    far_x, far_y = plane // ny, lax.rem(plane, ny)
    offset = (line // half_line) * sectors + lax.rem(line, half_line)
    far_at0 = jnp.where(near, -1, (far_y * nx + slot_of(far_x - x)) * half_line + offset)
    far_at1 = jnp.where(near, -1, (far_x * nx + slot_of(far_y - y)) * half_line + offset)
    targets = mt_v[...]
    mcolumns_v[...] = transposed([
        mg_v[...].astype(F32), near_at.astype(F32), targets.astype(F32), far_at0.astype(F32), far_at1.astype(F32),
    ])
    minc[...] = incidence(targets, ec_v[0, :, 1:2])

    columns = mcolumns_v[...]
    near_hot[...] = one_hot(columns[:, 4:5], 512)
    mbase[...] = dot(target_hot(columns), mtg_t[...])
    for g in range(2):
        far_hot[0, g] = one_hot(columns[:, 6:7] - g * sectors, sectors)
        far_hot[1, g] = one_hot(columns[:, 7:8] - g * sectors, sectors)
    mself_term = dot(encoded, pi_v[...])

    near_copies[0].wait_recv()
    near_copies[1].wait_recv()
    for k in (2, 3):
        guarded(sends(near_moves[k][3]), near_copies[k].start)

    def place_rows(which):
        row_at = lax.broadcasted_iota(I32, (half_line, LATENT), 0)
        block = jnp.zeros((half_line, LATENT), F32)
        for k in range(half_line):
            block = jnp.where(row_at == k, rows_in[which * half_line + k], block)
        half = jnp.where(core == 0, block[:, :HALF], block[:, HALF:])
        far_t[which, core, second, 0] = half.astype(BF16)

    def fixed_slot(step):
        return 0 if step == 0 else 2 * step - 1 if step <= nx // 2 else 2 * (nx - step)

    def stage2(turn, which, k):
        slot = fixed_slot(nx - k)
        return pltpu.make_async_remote_copy(
            src_ref=far_t.at[which, core, second, 0], dst_ref=far_t.at[which, core, second, slot],
            send_sem=s2_ss.at[turn, slot], recv_sem=s2_rs.at[turn, slot], device_id=first_peer(k), device_id_type=MESH,
        )

    parts = [(0, 3), (3, 5), (5, 7), (7, 8)] if nx == 8 else [(0, 1), (1, nx)]

    def stage3(turn, which, part, k, source):
        low, high = parts[part]
        at = far_t.at[which, core, source, pl.ds(low, high - low)]
        return pltpu.make_async_remote_copy(
            src_ref=at, dst_ref=at, send_sem=s3_ss.at[turn, part, k], recv_sem=s3_rs.at[turn, part, source],
            device_id=second_peer(k), device_id_type=MESH,
        )

    def stage4(turn, which, half_of, source):
        at = far_t.at[which, half_of, source]
        return pltpu.make_async_remote_copy(
            src_ref=at, dst_ref=at, send_sem=s4_ss.at[turn, source], recv_sem=s4_rs.at[turn, source],
            device_id=(lon, lat + 1 - 2 * core), device_id_type=MESH,
        )

    order = sorted(range(1, nx), key=lambda k: min(k, nx - k))

    def start2(turn, which):
        for k in range(1, nx):
            stage2(turn, which, k).start()

    def start3(turn, which):
        for part, (low, high) in enumerate(parts):
            for k in range(1, nx):
                if low <= fixed_slot(nx - k) < high:
                    stage2(turn, which, k).wait_recv()
            for k in reversed(order):
                stage3(turn, which, part, k, second).start()
        stage4(turn, which, core, second).start()

    def hand_on(turn, which):
        for k in order:
            source = lax.rem(second + k, nx)
            for part in range(len(parts)):
                stage3(turn, which, part, k, source).wait_recv()
            stage4(turn, which, core, source).start()

    def wait4(turn, which):
        for k in range(nx):
            stage4(turn, which, 1 - core, k).wait_recv()

    def far_part(which):
        parts = [dot(far_hot[h, which], far_t[which, h].reshape(sectors, HALF)) for h in range(2)]
        return jnp.concatenate(parts, axis=1)

    def wait_row(k, carry):
        line_arrival(k).wait_recv()
        return carry

    lax.fori_loop(group * half_line, lat, wait_row, 0)
    lax.fori_loop(lat + 1, (group + 1) * half_line, wait_row, 0)
    place_rows(group)
    later = 2 * (nx - 1) - ranked(x) - ranked(y)

    @pl.when(later > 0)
    def _():
        pl.semaphore_wait(late_plane, later)

    start2(0, group)

    @pl.when(group == 0)
    def _():
        pl.semaphore_wait(late_other, half_line)
        lax.fori_loop(half_line, nlat, send_row, 0)

    lax.fori_loop(other * half_line, (other + 1) * half_line, wait_row, 0)
    place_rows(other)
    start2(1, other)
    start3(0, group)
    for k in (2, 3):
        guarded(receives(near_moves[k][3]), near_copies[k].wait_recv)
    mbase[...] += dot(near_hot[...], near_t[...])
    start3(1, other)
    hand_on(0, group)
    wait4(0, group)
    mbase[...] += far_part(group)
    hand_on(1, other)
    wait4(1, other)
    hidden = silu(mbase[...] + far_part(other)).astype(BF16)
    message = layer_norm(dot(hidden, po_v[...])).astype(BF16)
    minflow = dot(minc[...], message).astype(BF16)
    hidden = silu(mself_term + dot(minflow, pin_v[...])).astype(BF16)
    update = layer_norm(dot(hidden, pf_v[...]))
    out_ref[0, 0] = (encoded.astype(F32) + update).astype(BF16)

    for copy, (*_, step) in zip(halo_copies, halo_moves):
        guarded(sends(step), copy.wait_send)
    for copy, (*_, step) in zip(near_copies, near_moves):
        guarded(sends(step), copy.wait_send)

    def end_row(k, carry):
        line_copy(k).wait_send()
        return carry

    lax.fori_loop(0, lat, end_row, 0)
    lax.fori_loop(lat + 1, nlat, end_row, 0)
    for turn, which in ((0, group), (1, other)):
        for k in range(1, nx):
            stage2(turn, which, k).wait_send()
            for part in range(len(parts)):
                stage3(turn, which, part, k, second).wait_send()
        for k in range(nx):
            stage4(turn, which, core, k).wait_send()


def body(nx, ny, nlat, *args):
    weight = pltpu.VMEM((LATENT, LATENT), BF16)
    narrow = pltpu.VMEM((4, LATENT), BF16)
    half_line = nlat // 2
    sectors = nx * ny * half_line
    dma = pltpu.SemaphoreType.DMA
    scratch = [
        pltpu.VMEM((GRID_LAT, GRID_LON, LATENT), BF16), pltpu.VMEM((SLOTS, LATENT), BF16),
        pltpu.VMEM((1, GRID_EDGES), I32), pltpu.VMEM((1, GRID_EDGES), I32), pltpu.VMEM((4, GRID_EDGES), BF16),
        pltpu.VMEM((1, MESH_EDGES), I32), pltpu.VMEM((1, MESH_EDGES), I32), pltpu.VMEM((4, MESH_EDGES), BF16),
        pltpu.VMEM((1, 1, 2), I32),
        weight, weight, narrow, weight, weight, weight, weight,
        weight, weight, narrow, weight, weight, weight, weight,
        pltpu.VMEM((OWN, LATENT), BF16), pltpu.VMEM((PACKED, LATENT), BF16), pltpu.VMEM((RIM, GRID_LON, LATENT), BF16),
        pltpu.VMEM((RIM, GRID_LON, LATENT), BF16), pltpu.VMEM((PACKED + 32, LATENT), BF16), pltpu.VMEM((HALO, LATENT), BF16),
        pltpu.VMEM((128, LATENT), BF16), pltpu.VMEM((GRID_EDGES, 8), F32), pltpu.VMEM((GRID_EDGES, HALO), BF16),
        pltpu.VMEM((GRID_EDGES, LATENT), F32), pltpu.VMEM((SLOTS, GRID_EDGES), BF16),
        pltpu.VMEM((512, LATENT), BF16),
        pltpu.VMEM((128, LATENT), BF16), pltpu.VMEM((MESH_EDGES, 8), F32), pltpu.VMEM((MESH_EDGES, 512), BF16),
        pltpu.VMEM((2, 2, MESH_EDGES, sectors), BF16),
        pltpu.VMEM((MESH_EDGES, LATENT), F32), pltpu.VMEM((SLOTS, MESH_EDGES), BF16),
        pltpu.VMEM((1, LATENT), F32), pltpu.VMEM((nlat, 1, LATENT), F32), pltpu.VMEM((2, 2, nx, nx, half_line, HALF), BF16),
        dma((23,)), pltpu.SemaphoreType.REGULAR, pltpu.SemaphoreType.REGULAR, pltpu.SemaphoreType.REGULAR, dma((8,)), dma((8,)), dma((4,)), dma((4,)), dma((nlat,)), dma((nlat,)),
        dma((2, nx)), dma((2, nx)), dma((2, 4, nx)), dma((2, 4, nx)), dma((2, nx)), dma((2, nx)),
    ]
    return pl.pallas_call(
        functools.partial(kernel, nx, ny, nlat),
        out_shape=pltpu.VMEM((1, 1, SLOTS, LATENT), BF16),
        in_specs=[pl.BlockSpec(memory_space=pl.ANY)] * 23,
        out_specs=pl.BlockSpec(memory_space=pltpu.VMEM),
        scratch_shapes=scratch,
        compiler_params=pltpu.CompilerParams(collective_id=0, has_side_effects=True, vmem_limit_bytes=60 * 2**20),
        cost_estimate=pl.CostEstimate(flops=3 * 10**9, bytes_accessed=6 * 10**6, transcendentals=10**6),
    )(*args[:8], jnp.transpose(args[8], (1, 2, 0)), *args[9:])


def solution(mesh):
    nlon, nlat = mesh.shape["lon"], mesh.shape["lat"]
    nx = round(nlon**0.5)
    return jax.shard_map(
        functools.partial(body, nx, nlon // nx, nlat),
        mesh=mesh,
        in_specs=(
            P("lat", "lon", None),
            P("lat", "lon", None, None),
            P("lat", "lon", None),
            P("lat", "lon", None),
            P("lat", "lon", None, None),
            P("lat", "lon", None),
            P("lat", "lon", None),
            P("lat", "lon", None, None),
            P(None, "lat", "lon"),
        )
        + (P(),) * 14,
        out_specs=P("lat", "lon", None, None),
        check_vma=False,
    )
```
